32 devices in a mesh: node: 8 (over z, x), local: 4 (over y, core).
Axes of the slice: x: 2, y: 2, z: 4, core: 2. Of those that a mesh axis runs over, the one named last changes fastest.
Arguments:
- tokens: bfloat16 [128, 4096], P('node', 'local'), may hold values from -6 to 6
- sign_bits: int32 [4096], P('local'), may hold values 0 or 1
- routes: int32 [128, 4], P('node'), may hold values from 0 to 7, all different within a row; in each aligned block of 16 rows (0 to 15, 16 to 31, ...) at most 16 rows name the same one
- gate_values: float32 [128, 4], P('node'), may hold values from 0.1 to 1
- gate_w: bfloat16 [8, 4096, 1024], P('node', 'local'), may hold values from -0.09375 to 0.09375
- up_w: bfloat16 [8, 4096, 1024], P('node', 'local'), may hold values from -0.09375 to 0.09375
- down_w: bfloat16 [8, 1024, 4096], P('node', None, 'local'), may hold values from -0.1875 to 0.1875
Outputs:
- mixed: bfloat16 [128, 4096], P('node', 'local')
The draws below stay inside these ranges and needn't reach their ends.
Inputs may be any that keep to these rules, and one draw needn't show every extreme that they name: `routes`: each row names 4 different experts; within the rows of one index of node (16 tokens, aligned blocks) no expert is named by more than 16 rows.
All inputs are finite; a program needn't handle non-finite values. No bound on the sum of `sign_bits` on one device may be relied on, other than what follows from the above.
Results may differ from the reference program's by a relative error of at most 0.0071.
Values may be sent and summed in bfloat16 or wider, within the bound.
A program may use at most 64 MiB of HBM per device.

```python
import math
import jax
import jax.numpy as jnp
import numpy as np
from jax import lax

D = 4096
FF = 1024
HB = 128
TOP = 4
TOK_NODE = 16
TOKENS = 128
EXPERTS = 8
CAP = 16
N_NODE = 8


def touch_ends(values, stream_key, least, largest):
    dims = values.shape
    place = [jax.random.randint(jax.random.fold_in(stream_key, axis), (), 0, dims[axis]) for axis in range(len(dims))]
    values = values.at[tuple(place)].set(least)
    longest = dims.index(max(dims))
    place[longest] = (place[longest] + 1) % dims[longest]
    return values.at[tuple(place)].set(largest)


def level_of(stream_key, extent, shards, low, largest):
    factor_of, own = 1.0, jax.random.fold_in(stream_key, 6)
    for dim, shards_of in shards:
        steps = jnp.exp(jax.random.uniform(jax.random.fold_in(own, dim), (shards_of,), jnp.float32, low / len(shards), largest / len(shards)))
        factor_of = factor_of * jnp.repeat(steps, extent[dim] // shards_of).reshape([-1 if axis == dim else 1 for axis in range(len(extent))])
    return factor_of


def deal_out(rng, own, number, rows, number_of, top, limit, skew):
    sequence = jax.random.permutation(rng, number_of)
    crowded, common = portions_of(number_of, rows * top, limit, skew, True), portions_of(number_of, rows * top, limit, skew, False)
    places = jnp.arange(number_of)

    def named(tallies, offset_by):
        used = int((tallies > 0).sum())
        fixed = max(1, used // 4)
        shifted = fixed + (places - fixed + offset_by * (used - fixed)) % max(1, number_of - fixed)
        return jnp.zeros((number_of,), jnp.int32).at[sequence[jnp.where(places < fixed, places, shifted)]].set(jnp.asarray(tallies, jnp.int32))

    tallies = jnp.where(number % 4 == 0, named(crowded, number // 4), named(common, number - number // 4 - 1))
    mixed = jax.random.permutation(jax.random.fold_in(own, 3), number_of)
    giver, sink = mixed[0:number_of // 2 * 2:2], mixed[1:number_of // 2 * 2:2]
    room = jnp.minimum(tallies[giver] - 1, limit - tallies[sink]) // 2
    room = jnp.where((giver == sequence[0]) | (sink == sequence[0]) | (tallies[sink] == 0), 0, jnp.maximum(room, 0))
    shifted = jax.random.randint(jax.random.fold_in(own, 4), (number_of // 2,), 0, 1 << 20) % (room + 1)
    tallies = tallies.at[giver].add(-shifted).at[sink].add(shifted)
    labels = jnp.searchsorted(jnp.cumsum(tallies), jnp.arange(rows * top), side="right").astype(jnp.int32)
    table = labels.reshape(top, rows).T
    table = table[jax.random.permutation(jax.random.fold_in(own, 1), rows)]
    offset_by = jax.random.randint(jax.random.fold_in(own, 2), (rows, 1), 0, top)
    return jnp.take_along_axis(table, (jnp.arange(top)[None, :] + offset_by) % top, axis=1)


def portions_of(number_of, total, most, skew, full):
    weights = [(1 << 20) // math.isqrt(grade ** skew) + 1 for grade in range(1, number_of + 1)]
    largest = most if full else min(most, max(-(-total // number_of), total * weights[0] // sum(weights)))
    least = 1 if total - largest >= number_of - 1 else 0
    counts, rest = [largest] + [least] * (number_of - 1), total - largest - least * (number_of - 1)
    while rest > 0:
        candidates = [i for i in range(1, number_of) if counts[i] < largest] or [i for i in range(1, number_of) if counts[i] < most]
        whole, remaining = sum([weights[i] for i in candidates]), rest
        for i in candidates:
            more = min(most - counts[i], max(1, remaining * weights[i] // whole), rest)
            counts[i] = counts[i] + more
            rest = rest - more
    return np.array(counts)


def centred(stream_key, dims, deviation, bound, cuts=(), kind=jnp.bfloat16):
    entries = jax.random.normal(stream_key, dims, jnp.float32) * deviation
    if len(cuts) > 0:
        entries = level_of(stream_key, dims, cuts, -0.22, 0.18) * entries
    return jnp.clip(entries, min=-bound, max=bound).astype(kind)


def setup_inputs(seed: int = 0) -> dict:
    key_list = jax.random.split(jax.random.key(seed), 8)
    tokens = centred(key_list[0], (TOKENS, D), 1.0, 6.0, ((0, 8), (1, 4)))
    sign_bits = touch_ends((jax.random.randint(key_list[1], (D,), 0, 2) < 1).astype(jnp.int32), jax.random.fold_in(key_list[1], 1), 0, 1)
    routes_keys = jax.random.split(jax.random.fold_in(key_list[2], 1), TOKENS // TOK_NODE)
    routes_turns = jax.random.permutation(jax.random.fold_in(key_list[2], 3), TOKENS // TOK_NODE)
    routes = jax.vmap(lambda own, number: deal_out(jax.random.fold_in(key_list[2], 2), own, number, TOK_NODE, EXPERTS, TOP, CAP, 2))(routes_keys, routes_turns).reshape((TOKENS, TOP))
    gate_values = jnp.clip(jnp.exp(math.log(1.0) - 2.3025851 * jax.random.uniform(key_list[3], (TOKENS, TOP), jnp.float32) ** level_of(key_list[3], (TOKENS, TOP), ((0, 8),), -0.2, 0.2)), 0.1, 1.0)
    gate_w = centred(key_list[4], (EXPERTS, D, FF), D ** -0.5, 0.09375, ((0, 8), (1, 4)))
    up_w = centred(key_list[5], (EXPERTS, D, FF), D ** -0.5, 0.09375, ((0, 8), (1, 4)))
    down_w = centred(key_list[6], (EXPERTS, FF, D), FF ** -0.5, 0.1875, ((0, 8), (2, 4)))
    return dict(tokens=tokens, sign_bits=sign_bits, routes=routes, gate_values=gate_values, gate_w=gate_w, up_w=up_w, down_w=down_w)


def hadamard_table(block_order):
    kernel_two = jnp.array([[1.0, 1.0], [1.0, -1.0]], jnp.float32)
    matrix = jnp.ones((1, 1), jnp.float32)
    while matrix.shape[0] < block_order:
        matrix = jnp.kron(matrix, kernel_two)
    return matrix / math.sqrt(block_order)

def run_expert(operands):
    rows_in, gate_mat, up_mat, down_mat = operands
    gate_act = jnp.dot(rows_in, gate_mat, preferred_element_type=jnp.float32)
    up_act = jnp.dot(rows_in, up_mat, preferred_element_type=jnp.float32)
    hidden = (jax.nn.silu(gate_act) * up_act).astype(jnp.bfloat16)
    return jnp.dot(hidden, down_mat, preferred_element_type=jnp.float32).astype(jnp.bfloat16)

def reference(tokens, sign_bits, routes, gate_values, gate_w, up_w, down_w):
    sign_vals = (1 - 2 * sign_bits).astype(jnp.float32)
    signed = tokens.astype(jnp.float32) * sign_vals[None, :]
    blocks = signed.reshape(TOKENS, D // HB, HB)
    rotated = jnp.einsum('tbj,jk->tbk', blocks, hadamard_table(HB), precision=lax.Precision.HIGHEST)
    rotated = rotated.reshape(TOKENS, D).astype(jnp.bfloat16)
    node_routes = routes.reshape(N_NODE, TOK_NODE * TOP)
    onehot = (node_routes[:, :, None] == jnp.arange(EXPERTS, dtype=jnp.int32)[None, None, :]).astype(jnp.int32)
    ranks = (lax.optimization_barrier(jnp.sum(jnp.cumsum(onehot, axis=1) * onehot, axis=2)) - 1).astype(jnp.int32)
    sources = jnp.arange(N_NODE, dtype=jnp.int32)[:, None]
    slot_index = (sources * CAP + ranks).astype(jnp.int32).reshape(TOKENS, TOP)
    repeated = jnp.repeat(rotated, TOP, axis=0)
    dispatched = jnp.zeros((EXPERTS, EXPERTS * CAP, D), jnp.bfloat16)
    dispatched = dispatched.at[routes.reshape(-1), slot_index.reshape(-1)].set(repeated)
    expert_out = lax.map(run_expert, (dispatched, gate_w, up_w, down_w))
    picked = expert_out[routes, slot_index]
    mixed = lax.optimization_barrier(jnp.sum(gate_values[:, :, None] * picked.astype(jnp.float32), axis=1))
    return mixed.astype(jnp.bfloat16)
```

```python
import functools
import math

import jax
import jax.numpy as jnp
from jax import lax
from jax.experimental import pallas as pl
from jax.experimental.pallas import tpu as pltpu
from jax.sharding import PartitionSpec as P

HB = 128
LANES = 128
CHUNKS = 4
MESH = pl.DeviceIdType.MESH


def fused_kernel(
    nodes,
    tok_ref, sign_ref, routes_ref, gv_ref, gw_hbm, uw_hbm, dw_hbm, out_ref,
    gw, uw, dw, arr, core_out, core_in, y_out, y_in, hid, acc, wf, x_out, x_in, z_own, z_out, z_in,
    w_sem, ag_send, ag_recv, fw_send, core_send, core_recv, y_send, y_recv,
    hid_send, hid_recv, x_send, x_recv, z_send, z_recv,
):
    rows, width = tok_ref.shape
    nz = nodes // 2
    total = nodes * rows
    half = total // 2
    piece = gw.shape[1] // 4
    cols = width // CHUNKS
    f32, bf16 = jnp.float32, jnp.bfloat16

    node = lax.axis_index("node")
    local = lax.axis_index("local")
    z, x = node // 2, node % 2
    y, c = local // 2, local % 2
    x_peer = {"node": z * 2 + (1 - x)}
    z_peers = [(z + step) % nz for step in range(1, nz)]
    core_peer_l = y * 2 + (1 - c)
    y_peer_l = (1 - y) * 2 + c
    core_peer = {"local": core_peer_l}
    y_peer = {"local": y_peer_l}

    loads = []
    for i, (src, dst) in enumerate(((gw_hbm, gw), (uw_hbm, uw), (dw_hbm, dw))):
        load = pltpu.make_async_copy(src.at[0], dst, w_sem.at[i])
        load.start()
        loads.append(load)

    barrier = pltpu.get_barrier_semaphore()
    peers = [x_peer, core_peer, y_peer] + [{"node": pz * 2 + x} for pz in z_peers]
    for peer in peers:
        pl.semaphore_signal(barrier, inc=1, device_id=peer, device_id_type=MESH)

    row_id = lax.broadcasted_iota(jnp.int32, (HB, HB), 0)
    col_id = lax.broadcasted_iota(jnp.int32, (HB, HB), 1)
    bits = row_id & col_id
    bits = bits ^ (bits >> 4)
    bits = bits ^ (bits >> 2)
    bits = bits ^ (bits >> 1)
    table = (1 - 2 * (bits & 1)).astype(f32).astype(bf16)
    me = x * nz + z
    signs = (1 - 2 * sign_ref[...]).astype(f32)
    signed = (tok_ref[...].astype(f32) * signs).astype(bf16)
    for b in range(width // HB):
        block = jnp.dot(signed[:, b * HB : (b + 1) * HB], table, preferred_element_type=f32)
        arr[me, :, b * HB : (b + 1) * HB] = (block * (1.0 / math.sqrt(HB))).astype(bf16)
    lane = lax.broadcasted_iota(jnp.int32, (rows, LANES), 1)
    dense = jnp.zeros((rows, LANES), f32)
    for k in range(routes_ref.shape[1]):
        hit = (lane % nodes) == routes_ref[:, k : k + 1]
        dense = dense + jnp.where(hit, gv_ref[:, k : k + 1], 0.0)
    high = dense.astype(bf16).astype(f32)
    middle = (dense - high).astype(bf16).astype(f32)
    low = dense - high - middle
    parts = jnp.where(lane < nodes, high, jnp.where(lane < 2 * nodes, middle, low))
    parts = jnp.where(lane < 3 * nodes, parts, 0.0)
    arr[me, :, width:] = parts.astype(bf16)

    pl.semaphore_wait(barrier, len(peers))

    def gather(slot, send_sem, peer):
        return pltpu.make_async_remote_copy(
            src_ref=arr.at[slot], dst_ref=arr.at[slot], send_sem=send_sem,
            recv_sem=ag_recv.at[slot], device_id=peer, device_id_type=MESH,
        )

    sent = []
    for i, pz in enumerate(z_peers):
        copy = gather(me, ag_send.at[i], {"node": pz * 2 + x})
        copy.start()
        sent.append(copy)
    copy = gather(me, fw_send.at[nz - 1], x_peer)
    copy.start()
    sent.append(copy)
    for i, pz in enumerate(z_peers):
        copy = gather(x * nz + pz, fw_send.at[i], x_peer)
        copy.wait_recv()
        copy.start()
        sent.append(copy)
    for pz in [z] + z_peers:
        gather((1 - x) * nz + pz, fw_send.at[0], x_peer).wait_recv()

    loads[0].wait()
    loads[1].wait()

    def partial_sums(p):
        where = pl.ds(pl.multiple_of(p * piece, piece), piece)
        tokens = arr[:, :, :width].reshape(total, width)
        gate = jnp.dot(tokens, gw[:, where], preferred_element_type=f32)
        up = jnp.dot(tokens, uw[:, where], preferred_element_type=f32)
        return gate, up

    def push(src, dst, send_sem, recv_sem, peer):
        copy = pltpu.make_async_remote_copy(
            src_ref=src, dst_ref=dst, send_sem=send_sem, recv_sem=recv_sem,
            device_id=peer, device_id_type=MESH,
        )
        copy.start()
        sent.append(copy)
        return copy

    def to_core(i, p):
        gate, up = partial_sums(p)
        core_out[i, :, :piece] = gate.astype(bf16)
        core_out[i, :, piece:] = up.astype(bf16)
        return push(core_out.at[i], core_in.at[i], core_send.at[i], core_recv.at[i], core_peer)

    first = to_core(0, (1 - y) * 2 + (1 - c))
    gate, up = partial_sums((1 - y) * 2 + c)
    first.wait_recv()
    y_out[:, :piece] = (gate + core_in[0, :, :piece].astype(f32)).astype(bf16)
    y_out[:, piece:] = (up + core_in[0, :, piece:].astype(f32)).astype(bf16)
    over_y = push(y_out, y_in, y_send.at[0], y_recv.at[0], y_peer)
    second = to_core(1, y * 2 + (1 - c))
    gate, up = partial_sums(local)
    second.wait_recv()
    gate = gate + core_in[1, :, :piece].astype(f32)
    up = up + core_in[1, :, piece:].astype(f32)
    over_y.wait_recv()
    gate = gate + y_in[:, :piece].astype(f32)
    up = up + y_in[:, piece:].astype(f32)
    hid[local] = (gate / (1.0 + jnp.exp(-gate)) * up).astype(bf16)

    def spread(p, i, peer):
        return pltpu.make_async_remote_copy(
            src_ref=hid.at[p], dst_ref=hid.at[p], send_sem=hid_send.at[i],
            recv_sem=hid_recv.at[p], device_id=peer, device_id_type=MESH,
        )

    for i, peer in enumerate((y_peer, core_peer)):
        copy = spread(local, i, peer)
        copy.start()
        sent.append(copy)
    loads[2].wait()

    def down(p, where):
        depth = pl.ds(pl.multiple_of(p * piece, piece), piece)
        return jnp.dot(hid[p], dw[depth, where], preferred_element_type=f32)

    chunk_at = [slice(j * cols, (j + 1) * cols) for j in range(CHUNKS)]
    for where in chunk_at:
        acc[:, where] = down(local, where)
    spread(core_peer_l, 0, core_peer).wait_recv()
    for where in chunk_at:
        acc[:, where] += down(core_peer_l, where)
    copy = spread(y_peer_l, 2, core_peer)
    copy.wait_recv()
    copy.start()
    sent.append(copy)
    for where in chunk_at:
        acc[:, where] += down(y_peer_l, where)
    last_l = (1 - y) * 2 + (1 - c)
    spread(last_l, 0, core_peer).wait_recv()

    lane = lax.broadcasted_iota(jnp.int32, (total, LANES), 1)
    mine = (lane == node) | (lane == node + nodes) | (lane == node + 2 * nodes)
    coded = arr[:, :, width:].reshape(total, LANES).astype(f32)
    weight = jnp.sum(jnp.where(mine, coded, 0.0), axis=1, keepdims=True)

    over_x = []
    for j, where in enumerate(chunk_at):
        result = (acc[:, where] + down(last_l, where)).astype(bf16).astype(f32)
        weighted = (result * weight).reshape(2, half, cols)
        wf[j] = weighted
        x_out[j] = weighted.astype(bf16)
        over_x.append(push(x_out.at[j, 1 - x], x_in.at[j], x_send.at[j], x_recv.at[j], x_peer))
    for j, where in enumerate(chunk_at):
        over_x[j].wait_recv()
        summed = (wf[j, x] + x_in[j].astype(f32)).reshape(nz, rows, cols)
        z_own[j] = summed
        z_out[j] = summed.astype(bf16)
        for i, pz in enumerate(z_peers):
            push(z_out.at[j, pz], z_in.at[j, i], z_send.at[j, i], z_recv.at[j, i], {"node": pz * 2 + x})
    for j, where in enumerate(chunk_at):
        mixed = z_own[j, z]
        for i in range(nz - 1):
            pltpu.make_async_remote_copy(
                src_ref=z_out.at[j, z], dst_ref=z_in.at[j, i], send_sem=z_send.at[j, i],
                recv_sem=z_recv.at[j, i], device_id=x_peer, device_id_type=MESH,
            ).wait_recv()
            mixed = mixed + z_in[j, i].astype(f32)
        out_ref[:, where] = mixed.astype(bf16)

    for copy in sent:
        copy.wait_send()


def fused(tokens, sign_bits, routes, gate_values, gate_w, up_w, down_w):
    nodes = lax.axis_size("node")
    rows, width = tokens.shape
    hidden = gate_w.shape[2]
    total, nz, piece, cols = nodes * rows, nodes // 2, hidden // 4, width // CHUNKS
    bf16, f32 = jnp.bfloat16, jnp.float32
    dma = pltpu.SemaphoreType.DMA
    vmem = pl.BlockSpec(memory_space=pltpu.VMEM)
    hbm = pl.BlockSpec(memory_space=pl.ANY)
    return pl.pallas_call(
        functools.partial(fused_kernel, nodes),
        out_shape=jax.ShapeDtypeStruct((rows, width), bf16),
        in_specs=[vmem] * 4 + [hbm] * 3,
        out_specs=vmem,
        scratch_shapes=[
            pltpu.VMEM((width, hidden), bf16),
            pltpu.VMEM((width, hidden), bf16),
            pltpu.VMEM((hidden, width), bf16),
            pltpu.VMEM((nodes, rows, width + LANES), bf16),
            pltpu.VMEM((2, total, 2 * piece), bf16),
            pltpu.VMEM((2, total, 2 * piece), bf16),
            pltpu.VMEM((total, 2 * piece), bf16),
            pltpu.VMEM((total, 2 * piece), bf16),
            pltpu.VMEM((4, total, piece), bf16),
            pltpu.VMEM((total, width), f32),
            pltpu.VMEM((CHUNKS, 2, total // 2, cols), f32),
            pltpu.VMEM((CHUNKS, 2, total // 2, cols), bf16),
            pltpu.VMEM((CHUNKS, total // 2, cols), bf16),
            pltpu.VMEM((CHUNKS, nz, rows, cols), f32),
            pltpu.VMEM((CHUNKS, nz, rows, cols), bf16),
            pltpu.VMEM((CHUNKS, nz - 1, rows, cols), bf16),
            dma((3,)),
            dma((nz - 1,)), dma((nodes,)), dma((nz,)),
            dma((2,)), dma((2,)), dma((1,)), dma((1,)),
            dma((3,)), dma((4,)),
            dma((CHUNKS,)), dma((CHUNKS,)),
            dma((CHUNKS, nz - 1)), dma((CHUNKS, nz - 1)),
        ],
        compiler_params=pltpu.CompilerParams(
            collective_id=0, has_side_effects=True, vmem_limit_bytes=48 * 1024 * 1024
        ),
        cost_estimate=pl.CostEstimate(
            flops=6 * total * width * hidden, bytes_accessed=6 * width * hidden, transcendentals=0
        ),
    )(tokens, sign_bits.reshape(1, width), routes, gate_values, gate_w, up_w, down_w)


def fits_fused(tokens, routes, gate_w, capacity):
    nodes, rows = lax.axis_size("node"), tokens.shape[0]
    return (
        capacity >= rows
        and nodes % 2 == 0
        and 4 <= nodes <= 16
        and lax.axis_size("local") == 4
        and rows % 16 == 0
        and nodes * rows <= 256
        and tokens.shape[1] % (CHUNKS * LANES) == 0
        and gate_w.shape[2] % (4 * LANES) == 0
    )


def hadamard_table(block_order):
    kernel_two = jnp.array([[1.0, 1.0], [1.0, -1.0]], jnp.float32)
    matrix = jnp.ones((1, 1), jnp.float32)
    while matrix.shape[0] < block_order:
        matrix = jnp.kron(matrix, kernel_two)
    return matrix / math.sqrt(block_order)


def slot_table(routes, experts, capacity):
    rows_all = routes.shape[0] * routes.shape[1]
    flat_routes = routes.reshape(rows_all)
    onehot = (flat_routes[:, None] == jnp.arange(experts, dtype=jnp.int32)[None, :]).astype(
        jnp.int32
    )
    ranks = jnp.sum(jnp.cumsum(onehot, axis=0) * onehot, axis=1) - 1
    slot_ids = flat_routes * capacity + ranks
    return slot_ids[None, :] == jnp.arange(experts * capacity, dtype=jnp.int32)[:, None]


def per_device(tokens, sign_bits, routes, gate_values, gate_w, up_w, down_w):
    experts = lax.axis_size("node")
    tok_node, width_dev = tokens.shape
    top_count = routes.shape[1]
    capacity = max(2, 2 * tok_node * top_count // experts)
    if fits_fused(tokens, routes, gate_w, capacity):
        return fused(tokens, sign_bits, routes, gate_values, gate_w, up_w, down_w)
    placed = slot_table(routes, experts, capacity).reshape(experts * capacity, tok_node, top_count)
    scatter_mat = jnp.any(placed, axis=2).astype(jnp.bfloat16)
    combine_mat = jnp.sum(placed.astype(jnp.float32) * gate_values[None, :, :], axis=2)
    hadamard = hadamard_table(HB)
    sign_vals = (1 - 2 * sign_bits).astype(jnp.float32)
    signed = tokens.astype(jnp.float32) * sign_vals[None, :]
    block_count = width_dev // HB
    group_size = min(2, block_count)
    group_width = group_size * HB
    received = []
    for group_index in range(block_count // group_size):
        rotated_parts = []
        for inner_index in range(group_size):
            first_col = group_index * group_width + inner_index * HB
            feature_block = signed[:, first_col : first_col + HB]
            rotated_parts.append(
                jnp.dot(feature_block, hadamard, precision=lax.Precision.HIGHEST).astype(
                    jnp.bfloat16
                )
            )
        rotated = jnp.concatenate(rotated_parts, axis=1)
        outgoing = jnp.dot(scatter_mat, rotated, preferred_element_type=jnp.float32).astype(
            jnp.bfloat16
        )
        received.append(lax.all_to_all(outgoing, "node", split_axis=0, concat_axis=0, tiled=True))
    arrived = jnp.concatenate(received, axis=1)
    gate_part = jnp.dot(arrived, gate_w[0], preferred_element_type=jnp.float32)
    up_part = jnp.dot(arrived, up_w[0], preferred_element_type=jnp.float32)
    gate_full, up_full = lax.psum((gate_part, up_part), "local")
    hidden_full = (jax.nn.silu(gate_full) * up_full).astype(jnp.bfloat16)
    expert_sum = jnp.dot(hidden_full, down_w[0], preferred_element_type=jnp.float32)
    expert_out = expert_sum.astype(jnp.bfloat16)
    combine_left = combine_mat.T
    mixed_blocks = []
    for group_index in range(block_count // group_size):
        out_block = expert_out[:, group_index * group_width : (group_index + 1) * group_width]
        returned_rows = lax.all_to_all(out_block, "node", split_axis=0, concat_axis=0, tiled=True)
        mixed_blocks.append(
            jnp.dot(
                combine_left, returned_rows.astype(jnp.float32), precision=lax.Precision.HIGHEST
            )
        )
    return jnp.concatenate(mixed_blocks, axis=1).astype(jnp.bfloat16)


def solution(mesh):
    in_specs = (
        P("node", "local"),
        P("local"),
        P("node", None),
        P("node", None),
        P("node", "local", None),
        P("node", "local", None),
        P("node", None, "local"),
    )
    out_specs = P("node", "local")
    return jax.shard_map(
        per_device, mesh=mesh, in_specs=in_specs, out_specs=out_specs, check_vma=False
    )
```

```python
import functools
import math

import jax
import jax.numpy as jnp
from jax import lax
from jax.experimental import pallas as pl
from jax.experimental.pallas import tpu as pltpu
from jax.sharding import PartitionSpec as P

HB = 128
LANES = 128
CHUNKS = 4
VMEM_BYTES = 64 * 1024 * 1024
MESH = pl.DeviceIdType.MESH


def fused_kernel(
    nodes,
    tok_hbm, sign_hbm, routes_hbm, gv_hbm, gw_hbm, uw_hbm, dw_hbm, out_ref,
    tok_ref, sign_ref, routes_ref, gv_ref, gw, uw, dw, arr, core_out, core_in, y_out, y_in, hid, acc, wf, x_out, x_in, z_own, z_out, z_in,
    w_sem, ag_send, ag_recv, fw_send, core_send, core_recv, y_send, y_recv,
    hid_send, hid_recv, x_send, x_recv, z_send, z_recv,
):
    rows, width = tok_hbm.shape
    nz = nodes // 2
    total = nodes * rows
    half = total // 2
    piece = gw.shape[1] // 4
    cols = width // CHUNKS
    f32, bf16 = jnp.float32, jnp.bfloat16

    node = lax.axis_index("node")
    local = lax.axis_index("local")
    z, x = node // 2, node % 2
    y, c = local // 2, local % 2
    x_peer = {"node": z * 2 + (1 - x)}
    z_peers = [(z + step) % nz for step in range(1, nz)]
    core_peer_l = y * 2 + (1 - c)
    y_peer_l = (1 - y) * 2 + c
    core_peer = {"local": core_peer_l}
    y_peer = {"local": y_peer_l}

    barrier = pltpu.get_barrier_semaphore()
    peers = [x_peer, core_peer, y_peer] + [{"node": pz * 2 + x} for pz in z_peers]
    for peer in peers:
        pl.semaphore_signal(barrier, inc=1, device_id=peer, device_id_type=MESH)

    loads = []
    for i, (src, dst) in enumerate((
        (tok_hbm, tok_ref), (sign_hbm, sign_ref), (routes_hbm, routes_ref), (gv_hbm, gv_ref),
        (gw_hbm.at[0], gw), (uw_hbm.at[0], uw), (dw_hbm.at[0], dw),
    )):
        load = pltpu.make_async_copy(src, dst, w_sem.at[i])
        load.start()
        loads.append(load)

    row_id = lax.broadcasted_iota(jnp.int32, (HB, HB), 0)
    col_id = lax.broadcasted_iota(jnp.int32, (HB, HB), 1)
    bits = row_id & col_id
    bits = bits ^ (bits >> 4)
    bits = bits ^ (bits >> 2)
    bits = bits ^ (bits >> 1)
    table = (1 - 2 * (bits & 1)).astype(f32).astype(bf16)
    me = x * nz + z
    for load in loads[:4]:
        load.wait()
    signs = (1 - 2 * sign_ref[...]).astype(f32)
    signed = (tok_ref[...].astype(f32) * signs).astype(bf16)
    for b in range(width // HB):
        block = jnp.dot(signed[:, b * HB : (b + 1) * HB], table, preferred_element_type=f32)
        arr[me, :, b * HB : (b + 1) * HB] = (block * (1.0 / math.sqrt(HB))).astype(bf16)
    code = lax.broadcasted_iota(jnp.int32, (LANES, rows), 0)
    dense = jnp.zeros((LANES, rows), f32)
    for k in range(routes_ref.shape[0]):
        hit = (code % nodes) == routes_ref[k : k + 1, :]
        dense = dense + jnp.where(hit, gv_ref[k : k + 1, :], 0.0)
    high = dense.astype(bf16).astype(f32)
    middle = (dense - high).astype(bf16).astype(f32)
    low = dense - high - middle
    parts = jnp.where(code < nodes, high, jnp.where(code < 2 * nodes, middle, low))
    parts = jnp.where(code < 3 * nodes, parts, 0.0).astype(bf16)
    same = lax.broadcasted_iota(jnp.int32, (rows, rows), 0) == lax.broadcasted_iota(jnp.int32, (rows, rows), 1)
    turned = lax.dot_general(
        same.astype(f32).astype(bf16), parts, (((1,), (1,)), ((), ())), preferred_element_type=f32
    )
    arr[me, :, width:] = turned.astype(bf16)

    pl.semaphore_wait(barrier, len(peers))

    def gather(slot, send_sem, peer):
        return pltpu.make_async_remote_copy(
            src_ref=arr.at[slot], dst_ref=arr.at[slot], send_sem=send_sem,
            recv_sem=ag_recv.at[slot], device_id=peer, device_id_type=MESH,
        )

    sent = []
    for i, pz in enumerate(z_peers):
        copy = gather(me, ag_send.at[i], {"node": pz * 2 + x})
        copy.start()
        sent.append(copy)
    copy = gather(me, fw_send.at[nz - 1], x_peer)
    copy.start()
    sent.append(copy)
    for i, pz in enumerate(z_peers):
        copy = gather(x * nz + pz, fw_send.at[i], x_peer)
        copy.wait_recv()
        copy.start()
        sent.append(copy)
    for pz in [z] + z_peers:
        gather((1 - x) * nz + pz, fw_send.at[0], x_peer).wait_recv()

    loads[4].wait()
    loads[5].wait()

    def partial_sums(p):
        where = pl.ds(pl.multiple_of(p * piece, piece), piece)
        tokens = arr[:, :, :width].reshape(total, width)
        gate = jnp.dot(tokens, gw[:, where], preferred_element_type=f32)
        up = jnp.dot(tokens, uw[:, where], preferred_element_type=f32)
        return gate, up

    def push(src, dst, send_sem, recv_sem, peer):
        copy = pltpu.make_async_remote_copy(
            src_ref=src, dst_ref=dst, send_sem=send_sem, recv_sem=recv_sem,
            device_id=peer, device_id_type=MESH,
        )
        copy.start()
        sent.append(copy)
        return copy

    def to_core(i, p):
        gate, up = partial_sums(p)
        core_out[i, :, :piece] = gate.astype(bf16)
        core_out[i, :, piece:] = up.astype(bf16)
        return push(core_out.at[i], core_in.at[i], core_send.at[i], core_recv.at[i], core_peer)

    first = to_core(0, (1 - y) * 2 + (1 - c))
    gate, up = partial_sums((1 - y) * 2 + c)
    first.wait_recv()
    y_out[:, :piece] = (gate + core_in[0, :, :piece].astype(f32)).astype(bf16)
    y_out[:, piece:] = (up + core_in[0, :, piece:].astype(f32)).astype(bf16)
    over_y = push(y_out, y_in, y_send.at[0], y_recv.at[0], y_peer)
    second = to_core(1, y * 2 + (1 - c))
    gate, up = partial_sums(local)
    second.wait_recv()
    gate = gate + core_in[1, :, :piece].astype(f32)
    up = up + core_in[1, :, piece:].astype(f32)
    over_y.wait_recv()
    gate = gate + y_in[:, :piece].astype(f32)
    up = up + y_in[:, piece:].astype(f32)
    hid[local] = (gate / (1.0 + jnp.exp(-gate)) * up).astype(bf16)

    def spread(p, i, peer):
        return pltpu.make_async_remote_copy(
            src_ref=hid.at[p], dst_ref=hid.at[p], send_sem=hid_send.at[i],
            recv_sem=hid_recv.at[p], device_id=peer, device_id_type=MESH,
        )

    for i, peer in enumerate((y_peer, core_peer)):
        copy = spread(local, i, peer)
        copy.start()
        sent.append(copy)
    loads[6].wait()

    def down(p, where):
        depth = pl.ds(pl.multiple_of(p * piece, piece), piece)
        return jnp.dot(hid[p], dw[depth, where], preferred_element_type=f32)

    chunk_at = [slice(j * cols, (j + 1) * cols) for j in range(CHUNKS)]
    for where in chunk_at:
        acc[:, where] = down(local, where)
    spread(core_peer_l, 0, core_peer).wait_recv()
    for where in chunk_at:
        acc[:, where] += down(core_peer_l, where)
    copy = spread(y_peer_l, 2, core_peer)
    copy.wait_recv()
    copy.start()
    sent.append(copy)
    for where in chunk_at:
        acc[:, where] += down(y_peer_l, where)
    last_l = (1 - y) * 2 + (1 - c)
    spread(last_l, 0, core_peer).wait_recv()

    lane = lax.broadcasted_iota(jnp.int32, (total, LANES), 1)
    mine = (lane == node) | (lane == node + nodes) | (lane == node + 2 * nodes)
    coded = arr[:, :, width:].reshape(total, LANES).astype(f32)
    weight = jnp.sum(jnp.where(mine, coded, 0.0), axis=1, keepdims=True)

    over_x = []
    for j, where in enumerate(chunk_at):
        result = (acc[:, where] + down(last_l, where)).astype(bf16).astype(f32)
        weighted = (result * weight).reshape(2, half, cols)
        wf[j] = weighted
        x_out[j] = weighted.astype(bf16)
        over_x.append(push(x_out.at[j, 1 - x], x_in.at[j], x_send.at[j], x_recv.at[j], x_peer))
    for j, where in enumerate(chunk_at):
        over_x[j].wait_recv()
        summed = (wf[j, x] + x_in[j].astype(f32)).reshape(nz, rows, cols)
        z_own[j] = summed
        z_out[j] = summed.astype(bf16)
        for i, pz in enumerate(z_peers):
            push(z_out.at[j, pz], z_in.at[j, i], z_send.at[j, i], z_recv.at[j, i], {"node": pz * 2 + x})
    for j, where in enumerate(chunk_at):
        mixed = z_own[j, z]
        for i in range(nz - 1):
            pltpu.make_async_remote_copy(
                src_ref=z_out.at[j, z], dst_ref=z_in.at[j, i], send_sem=z_send.at[j, i],
                recv_sem=z_recv.at[j, i], device_id=x_peer, device_id_type=MESH,
            ).wait_recv()
            mixed = mixed + z_in[j, i].astype(f32)
        out_ref[:, where] = mixed.astype(bf16)

    for copy in sent:
        copy.wait_send()


def fused(tokens, sign_bits, routes, gate_values, gate_w, up_w, down_w):
    nodes = lax.axis_size("node")
    rows, width = tokens.shape
    hidden = gate_w.shape[2]
    total, nz, piece, cols = nodes * rows, nodes // 2, hidden // 4, width // CHUNKS
    bf16, f32 = jnp.bfloat16, jnp.float32
    dma = pltpu.SemaphoreType.DMA
    vmem = pl.BlockSpec(memory_space=pltpu.VMEM)
    hbm = pl.BlockSpec(memory_space=pl.ANY)
    return pl.pallas_call(
        functools.partial(fused_kernel, nodes),
        out_shape=jax.ShapeDtypeStruct((rows, width), bf16),
        in_specs=[hbm] * 7,
        out_specs=vmem,
        scratch_shapes=[
            pltpu.VMEM((rows, width), bf16),
            pltpu.VMEM((1, width), jnp.int32),
            pltpu.VMEM((routes.shape[1], rows), jnp.int32),
            pltpu.VMEM((routes.shape[1], rows), f32),
            pltpu.VMEM((width, hidden), bf16),
            pltpu.VMEM((width, hidden), bf16),
            pltpu.VMEM((hidden, width), bf16),
            pltpu.VMEM((nodes, rows, width + LANES), bf16),
            pltpu.VMEM((2, total, 2 * piece), bf16),
            pltpu.VMEM((2, total, 2 * piece), bf16),
            pltpu.VMEM((total, 2 * piece), bf16),
            pltpu.VMEM((total, 2 * piece), bf16),
            pltpu.VMEM((4, total, piece), bf16),
            pltpu.VMEM((total, width), f32),
            pltpu.VMEM((CHUNKS, 2, total // 2, cols), f32),
            pltpu.VMEM((CHUNKS, 2, total // 2, cols), bf16),
            pltpu.VMEM((CHUNKS, total // 2, cols), bf16),
            pltpu.VMEM((CHUNKS, nz, rows, cols), f32),
            pltpu.VMEM((CHUNKS, nz, rows, cols), bf16),
            pltpu.VMEM((CHUNKS, nz - 1, rows, cols), bf16),
            dma((7,)),
            dma((nz - 1,)), dma((nodes,)), dma((nz,)),
            dma((2,)), dma((2,)), dma((1,)), dma((1,)),
            dma((3,)), dma((4,)),
            dma((CHUNKS,)), dma((CHUNKS,)),
            dma((CHUNKS, nz - 1)), dma((CHUNKS, nz - 1)),
        ],
        compiler_params=pltpu.CompilerParams(
            collective_id=0, has_side_effects=True, vmem_limit_bytes=VMEM_BYTES
        ),
        cost_estimate=pl.CostEstimate(
            flops=6 * total * width * hidden, bytes_accessed=6 * width * hidden, transcendentals=0
        ),
    )(tokens, sign_bits.reshape(1, width), routes.T, gate_values.T, gate_w, up_w, down_w)


def fits_fused(tokens, routes, gate_w, capacity):
    nodes, rows = lax.axis_size("node"), tokens.shape[0]
    return (
        capacity >= rows
        and nodes % 2 == 0
        and 4 <= nodes <= 16
        and lax.axis_size("local") == 4
        and rows % 16 == 0
        and nodes * rows <= 256
        and tokens.shape[1] % (CHUNKS * LANES) == 0
        and gate_w.shape[2] % (4 * LANES) == 0
    )


def hadamard_table(block_order):
    kernel_two = jnp.array([[1.0, 1.0], [1.0, -1.0]], jnp.float32)
    matrix = jnp.ones((1, 1), jnp.float32)
    while matrix.shape[0] < block_order:
        matrix = jnp.kron(matrix, kernel_two)
    return matrix / math.sqrt(block_order)


def slot_table(routes, experts, capacity):
    rows_all = routes.shape[0] * routes.shape[1]
    flat_routes = routes.reshape(rows_all)
    onehot = (flat_routes[:, None] == jnp.arange(experts, dtype=jnp.int32)[None, :]).astype(
        jnp.int32
    )
    ranks = jnp.sum(jnp.cumsum(onehot, axis=0) * onehot, axis=1) - 1
    slot_ids = flat_routes * capacity + ranks
    return slot_ids[None, :] == jnp.arange(experts * capacity, dtype=jnp.int32)[:, None]


def per_device(tokens, sign_bits, routes, gate_values, gate_w, up_w, down_w):
    experts = lax.axis_size("node")
    tok_node, width_dev = tokens.shape
    top_count = routes.shape[1]
    capacity = max(2, 2 * tok_node * top_count // experts)
    if fits_fused(tokens, routes, gate_w, capacity):
        return fused(tokens, sign_bits, routes, gate_values, gate_w, up_w, down_w)
    placed = slot_table(routes, experts, capacity).reshape(experts * capacity, tok_node, top_count)
    scatter_mat = jnp.any(placed, axis=2).astype(jnp.bfloat16)
    combine_mat = jnp.sum(placed.astype(jnp.float32) * gate_values[None, :, :], axis=2)
    hadamard = hadamard_table(HB)
    sign_vals = (1 - 2 * sign_bits).astype(jnp.float32)
    signed = tokens.astype(jnp.float32) * sign_vals[None, :]
    block_count = width_dev // HB
    group_size = min(2, block_count)
    group_width = group_size * HB
    received = []
    for group_index in range(block_count // group_size):
        rotated_parts = []
        for inner_index in range(group_size):
            first_col = group_index * group_width + inner_index * HB
            feature_block = signed[:, first_col : first_col + HB]
            rotated_parts.append(
                jnp.dot(feature_block, hadamard, precision=lax.Precision.HIGHEST).astype(
                    jnp.bfloat16
                )
            )
        rotated = jnp.concatenate(rotated_parts, axis=1)
        outgoing = jnp.dot(scatter_mat, rotated, preferred_element_type=jnp.float32).astype(
            jnp.bfloat16
        )
        received.append(lax.all_to_all(outgoing, "node", split_axis=0, concat_axis=0, tiled=True))
    arrived = jnp.concatenate(received, axis=1)
    gate_part = jnp.dot(arrived, gate_w[0], preferred_element_type=jnp.float32)
    up_part = jnp.dot(arrived, up_w[0], preferred_element_type=jnp.float32)
    gate_full, up_full = lax.psum((gate_part, up_part), "local")
    hidden_full = (jax.nn.silu(gate_full) * up_full).astype(jnp.bfloat16)
    expert_sum = jnp.dot(hidden_full, down_w[0], preferred_element_type=jnp.float32)
    expert_out = expert_sum.astype(jnp.bfloat16)
    combine_left = combine_mat.T
    mixed_blocks = []
    for group_index in range(block_count // group_size):
        out_block = expert_out[:, group_index * group_width : (group_index + 1) * group_width]
        returned_rows = lax.all_to_all(out_block, "node", split_axis=0, concat_axis=0, tiled=True)
        mixed_blocks.append(
            jnp.dot(
                combine_left, returned_rows.astype(jnp.float32), precision=lax.Precision.HIGHEST
            )
        )
    return jnp.concatenate(mixed_blocks, axis=1).astype(jnp.bfloat16)


def solution(mesh):
    in_specs = (
        P("node", "local"),
        P("local"),
        P("node", None),
        P("node", None),
        P("node", "local", None),
        P("node", "local", None),
        P("node", None, "local"),
    )
    out_specs = P("node", "local")
    return jax.shard_map(
        per_device, mesh=mesh, in_specs=in_specs, out_specs=out_specs, check_vma=False
    )
```

```python
import functools
import math

import jax
import jax.numpy as jnp
from jax import lax
from jax.experimental import pallas as pl
from jax.experimental.pallas import tpu as pltpu
from jax.sharding import PartitionSpec as P

HB = 128
LANES = 128
CHUNKS = 2
VMEM_BYTES = 63 * 1024 * 1024
MESH = pl.DeviceIdType.MESH


def fused_kernel(
    nodes,
    tok_hbm, sign_hbm, routes_hbm, gv_hbm, gw_hbm, uw_hbm, dw_hbm, out_ref,
    tok_ref, sign_ref, routes_ref, gv_ref, gw, uw, dw, arr,
    core_out, core_in, y_out, y_in, hid, acc, own, back_out, back_in,
    w_sem, ag_send, ag_recv, fw_send, core_send, core_recv, y_send, y_recv,
    hid_send, hid_recv, back_send, back_recv,
):
    rows, width = tok_hbm.shape
    nz = nodes // 2
    half = nz * rows
    piece = gw.shape[1] // 4
    cols = width // CHUNKS
    f32, bf16 = jnp.float32, jnp.bfloat16

    node = lax.axis_index("node")
    local = lax.axis_index("local")
    z, x = node // 2, node % 2
    y, c = local // 2, local % 2
    x_peer = {"node": z * 2 + (1 - x)}
    z_peers = [(z + step) % nz for step in range(1, nz)]
    core_peer_l, y_peer_l, far_l = y * 2 + (1 - c), (1 - y) * 2 + c, (1 - y) * 2 + (1 - c)
    core_peer, y_peer, far_peer = {"local": core_peer_l}, {"local": y_peer_l}, {"local": far_l}
    same_plane = [{"node": pz * 2 + x} for pz in z_peers]
    other_plane = [{"node": pz * 2 + (1 - x)} for pz in [z] + z_peers]

    barrier = pltpu.get_barrier_semaphore()
    peers = [core_peer, y_peer, far_peer] + same_plane + other_plane
    for peer in peers:
        pl.semaphore_signal(barrier, inc=1, device_id=peer, device_id_type=MESH)

    loads = []
    for i, (src, dst) in enumerate((
        (tok_hbm, tok_ref), (sign_hbm, sign_ref), (routes_hbm, routes_ref), (gv_hbm, gv_ref),
        (gw_hbm.at[0], gw), (uw_hbm.at[0], uw), (dw_hbm.at[0], dw),
    )):
        load = pltpu.make_async_copy(src, dst, w_sem.at[i])
        load.start()
        loads.append(load)

    row_id = lax.broadcasted_iota(jnp.int32, (HB, HB), 0)
    col_id = lax.broadcasted_iota(jnp.int32, (HB, HB), 1)
    bits = row_id & col_id
    bits = bits ^ (bits >> 4)
    bits = bits ^ (bits >> 2)
    bits = bits ^ (bits >> 1)
    table = (1 - 2 * (bits & 1)).astype(f32).astype(bf16)
    for load in loads[:4]:
        load.wait()
    signs = (1 - 2 * sign_ref[...]).astype(f32)
    signed = (tok_ref[...].astype(f32) * signs).astype(bf16)
    for b in range(width // HB):
        block = jnp.dot(signed[:, b * HB : (b + 1) * HB], table, preferred_element_type=f32)
        arr[x, z, :, b * HB : (b + 1) * HB] = (block * (1.0 / math.sqrt(HB))).astype(bf16)
    code = lax.broadcasted_iota(jnp.int32, (LANES, rows), 0)
    dense = jnp.zeros((LANES, rows), f32)
    for k in range(routes_ref.shape[0]):
        hit = (code % nodes) == routes_ref[k : k + 1, :]
        dense = dense + jnp.where(hit, gv_ref[k : k + 1, :], 0.0)
    high = dense.astype(bf16).astype(f32)
    middle = (dense - high).astype(bf16).astype(f32)
    low = dense - high - middle
    parts = jnp.where(code < nodes, high, jnp.where(code < 2 * nodes, middle, low))
    parts = jnp.where(code < 3 * nodes, parts, 0.0).astype(bf16)
    same = lax.broadcasted_iota(jnp.int32, (rows, rows), 0) == lax.broadcasted_iota(jnp.int32, (rows, rows), 1)
    turned = lax.dot_general(
        same.astype(f32).astype(bf16), parts, (((1,), (1,)), ((), ())), preferred_element_type=f32
    )
    arr[x, z, :, width:] = turned.astype(bf16)

    pl.semaphore_wait(barrier, len(peers))

    def gather(plane, pz, send_sem, peer):
        return pltpu.make_async_remote_copy(
            src_ref=arr.at[plane, pz], dst_ref=arr.at[plane, pz], send_sem=send_sem,
            recv_sem=ag_recv.at[plane, pz], device_id=peer, device_id_type=MESH,
        )

    sent = []

    def start(copy):
        copy.start()
        sent.append(copy)
        return copy

    def push(src, dst, send_sem, recv_sem, peer):
        return start(pltpu.make_async_remote_copy(
            src_ref=src, dst_ref=dst, send_sem=send_sem, recv_sem=recv_sem,
            device_id=peer, device_id_type=MESH,
        ))

    for i, peer in enumerate(same_plane):
        start(gather(x, z, ag_send.at[i], peer))
    start(gather(x, z, fw_send.at[nz - 1], x_peer))
    for i, pz in enumerate(z_peers):
        copy = gather(x, pz, fw_send.at[i], x_peer)
        copy.wait_recv()
        start(copy)
    loads[4].wait()
    loads[5].wait()

    planes = (x, 1 - x)

    def partial_sums(group, p):
        where = pl.ds(pl.multiple_of(p * piece, piece), piece)
        tokens = arr[planes[group], :, :, :width].reshape(half, width)
        gate = jnp.dot(tokens, gw[:, where], preferred_element_type=f32)
        up = jnp.dot(tokens, uw[:, where], preferred_element_type=f32)
        return gate, up

    def to_core(i, group, p):
        gate, up = partial_sums(group, p)
        core_out[i, :, :piece] = gate.astype(bf16)
        core_out[i, :, piece:] = up.astype(bf16)
        return push(core_out.at[i], core_in.at[i], core_send.at[i], core_recv.at[i], core_peer)

    def add_core(i, copy, gate, up):
        copy.wait_recv()
        return gate + core_in[i, :, :piece].astype(f32), up + core_in[i, :, piece:].astype(f32)

    def to_y(group):
        copy = to_core(group, group, far_l)
        gate, up = add_core(group, copy, *partial_sums(group, y_peer_l))
        y_out[group, :, :piece] = gate.astype(bf16)
        y_out[group, :, piece:] = up.astype(bf16)
        return push(y_out.at[group], y_in.at[group], y_send.at[group], y_recv.at[group], y_peer)

    def spread(group, p, i, peer):
        return pltpu.make_async_remote_copy(
            src_ref=hid.at[group, p], dst_ref=hid.at[group, p], send_sem=hid_send.at[group, i],
            recv_sem=hid_recv.at[group, p], device_id=peer, device_id_type=MESH,
        )

    def activate(group, gate, up, over_y):
        over_y.wait_recv()
        gate = gate + y_in[group, :, :piece].astype(f32)
        up = up + y_in[group, :, piece:].astype(f32)
        hid[group, local] = (gate / (1.0 + jnp.exp(-gate)) * up).astype(bf16)
        for i, peer in enumerate((y_peer, far_peer, core_peer)):
            start(spread(group, local, i, peer))

    over_y0 = to_y(0)
    for pz in [z] + z_peers:
        gather(1 - x, pz, fw_send.at[0], x_peer).wait_recv()
    over_y1 = to_y(1)
    near0 = to_core(2, 0, core_peer_l)
    gate0, up0 = partial_sums(0, local)
    near1 = to_core(3, 1, core_peer_l)
    activate(0, *add_core(2, near0, gate0, up0), over_y0)
    gate1, up1 = partial_sums(1, local)
    activate(1, *add_core(3, near1, gate1, up1), over_y1)
    loads[6].wait()

    chunk_at = [slice(j * cols, (j + 1) * cols) for j in range(CHUNKS)]

    def down(group, p, where):
        depth = pl.ds(pl.multiple_of(p * piece, piece), piece)
        return jnp.dot(hid[group, p], dw[depth, where], preferred_element_type=f32)

    lane = lax.broadcasted_iota(jnp.int32, (half, LANES), 1)
    mine = (lane == node) | (lane == node + nodes) | (lane == node + 2 * nodes)

    def give_back(group):
        for where in chunk_at:
            acc[group, :, where] = down(group, local, where)
        for p in (core_peer_l, y_peer_l):
            spread(group, p, 0, core_peer).wait_recv()
            for where in chunk_at:
                acc[group, :, where] += down(group, p, where)
        coded = arr[planes[group], :, :, width:].reshape(half, LANES).astype(f32)
        weight = jnp.sum(jnp.where(mine, coded, 0.0), axis=1, keepdims=True)
        spread(group, far_l, 0, core_peer).wait_recv()
        targets = ([z] + z_peers, other_plane) if group else (z_peers, same_plane)
        for j, where in enumerate(chunk_at):
            result = (acc[group, :, where] + down(group, far_l, where)).astype(bf16).astype(f32)
            weighted = (result * weight).reshape(nz, rows, cols)
            back_out[group, j] = weighted.astype(bf16)
            if group == 0:
                own[j] = weighted
            for i, (pz, peer) in enumerate(zip(*targets)):
                slot = i + group * (nz - 1)
                push(back_out.at[group, j, pz], back_in.at[j, slot],
                     back_send.at[j, slot], back_recv.at[j, slot], peer)

    give_back(0)
    give_back(1)

    for j, where in enumerate(chunk_at):
        mixed = own[j, z]
        for i in range(nodes - 1):
            pltpu.make_async_remote_copy(
                src_ref=back_out.at[0, j, 0], dst_ref=back_in.at[j, i], send_sem=back_send.at[j, i],
                recv_sem=back_recv.at[j, i], device_id=x_peer, device_id_type=MESH,
            ).wait_recv()
            mixed = mixed + back_in[j, i].astype(f32)
        out_ref[:, where] = mixed.astype(bf16)

    for copy in sent:
        copy.wait_send()


def fused(tokens, sign_bits, routes, gate_values, gate_w, up_w, down_w):
    nodes = lax.axis_size("node")
    rows, width = tokens.shape
    hidden = gate_w.shape[2]
    nz, piece, cols = nodes // 2, hidden // 4, width // CHUNKS
    total, half = nodes * rows, nz * rows
    bf16, f32 = jnp.bfloat16, jnp.float32
    dma = pltpu.SemaphoreType.DMA
    vmem = pl.BlockSpec(memory_space=pltpu.VMEM)
    hbm = pl.BlockSpec(memory_space=pltpu.HBM)
    return pl.pallas_call(
        functools.partial(fused_kernel, nodes),
        out_shape=pltpu.VMEM((rows, width), bf16),
        in_specs=[hbm] * 7,
        out_specs=vmem,
        scratch_shapes=[
            pltpu.VMEM((rows, width), bf16),
            pltpu.VMEM((1, width), jnp.int32),
            pltpu.VMEM((routes.shape[1], rows), jnp.int32),
            pltpu.VMEM((routes.shape[1], rows), f32),
            pltpu.VMEM((width, hidden), bf16),
            pltpu.VMEM((width, hidden), bf16),
            pltpu.VMEM((hidden, width), bf16),
            pltpu.VMEM((2, nz, rows, width + LANES), bf16),
            pltpu.VMEM((4, half, 2 * piece), bf16),
            pltpu.VMEM((4, half, 2 * piece), bf16),
            pltpu.VMEM((2, half, 2 * piece), bf16),
            pltpu.VMEM((2, half, 2 * piece), bf16),
            pltpu.VMEM((2, 4, half, piece), bf16),
            pltpu.VMEM((2, half, width), f32),
            pltpu.VMEM((CHUNKS, nz, rows, cols), f32),
            pltpu.VMEM((2, CHUNKS, nz, rows, cols), bf16),
            pltpu.VMEM((CHUNKS, nodes - 1, rows, cols), bf16),
            dma((7,)),
            dma((nz - 1,)), dma((2, nz)), dma((nz,)),
            dma((4,)), dma((4,)), dma((2,)), dma((2,)),
            dma((2, 3)), dma((2, 4)),
            dma((CHUNKS, nodes - 1)), dma((CHUNKS, nodes - 1)),
        ],
        compiler_params=pltpu.CompilerParams(
            collective_id=0, has_side_effects=True, vmem_limit_bytes=VMEM_BYTES
        ),
        cost_estimate=pl.CostEstimate(
            flops=6 * total * width * hidden, bytes_accessed=6 * width * hidden, transcendentals=0
        ),
    )(tokens, sign_bits.reshape(1, width), routes.T, gate_values.T, gate_w, up_w, down_w)


def fits_fused(tokens, routes, gate_w, capacity):
    nodes, rows = lax.axis_size("node"), tokens.shape[0]
    return (
        capacity >= rows
        and nodes % 2 == 0
        and 4 <= nodes <= 16
        and lax.axis_size("local") == 4
        and rows % 16 == 0
        and nodes * rows <= 256
        and tokens.shape[1] % (CHUNKS * LANES) == 0
        and gate_w.shape[2] % (4 * LANES) == 0
    )


def hadamard_table(block_order):
    kernel_two = jnp.array([[1.0, 1.0], [1.0, -1.0]], jnp.float32)
    matrix = jnp.ones((1, 1), jnp.float32)
    while matrix.shape[0] < block_order:
        matrix = jnp.kron(matrix, kernel_two)
    return matrix / math.sqrt(block_order)


def slot_table(routes, experts, capacity):
    rows_all = routes.shape[0] * routes.shape[1]
    flat_routes = routes.reshape(rows_all)
    onehot = (flat_routes[:, None] == jnp.arange(experts, dtype=jnp.int32)[None, :]).astype(
        jnp.int32
    )
    ranks = jnp.sum(jnp.cumsum(onehot, axis=0) * onehot, axis=1) - 1
    slot_ids = flat_routes * capacity + ranks
    return slot_ids[None, :] == jnp.arange(experts * capacity, dtype=jnp.int32)[:, None]


def per_device(tokens, sign_bits, routes, gate_values, gate_w, up_w, down_w):
    experts = lax.axis_size("node")
    tok_node, width_dev = tokens.shape
    top_count = routes.shape[1]
    capacity = max(2, 2 * tok_node * top_count // experts)
    if fits_fused(tokens, routes, gate_w, capacity):
        return fused(tokens, sign_bits, routes, gate_values, gate_w, up_w, down_w)
    placed = slot_table(routes, experts, capacity).reshape(experts * capacity, tok_node, top_count)
    scatter_mat = jnp.any(placed, axis=2).astype(jnp.bfloat16)
    combine_mat = jnp.sum(placed.astype(jnp.float32) * gate_values[None, :, :], axis=2)
    hadamard = hadamard_table(HB)
    sign_vals = (1 - 2 * sign_bits).astype(jnp.float32)
    signed = tokens.astype(jnp.float32) * sign_vals[None, :]
    block_count = width_dev // HB
    group_size = min(2, block_count)
    group_width = group_size * HB
    received = []
    for group_index in range(block_count // group_size):
        rotated_parts = []
        for inner_index in range(group_size):
            first_col = group_index * group_width + inner_index * HB
            feature_block = signed[:, first_col : first_col + HB]
            rotated_parts.append(
                jnp.dot(feature_block, hadamard, precision=lax.Precision.HIGHEST).astype(
                    jnp.bfloat16
                )
            )
        rotated = jnp.concatenate(rotated_parts, axis=1)
        outgoing = jnp.dot(scatter_mat, rotated, preferred_element_type=jnp.float32).astype(
            jnp.bfloat16
        )
        received.append(lax.all_to_all(outgoing, "node", split_axis=0, concat_axis=0, tiled=True))
    arrived = jnp.concatenate(received, axis=1)
    gate_part = jnp.dot(arrived, gate_w[0], preferred_element_type=jnp.float32)
    up_part = jnp.dot(arrived, up_w[0], preferred_element_type=jnp.float32)
    gate_full, up_full = lax.psum((gate_part, up_part), "local")
    hidden_full = (jax.nn.silu(gate_full) * up_full).astype(jnp.bfloat16)
    expert_sum = jnp.dot(hidden_full, down_w[0], preferred_element_type=jnp.float32)
    expert_out = expert_sum.astype(jnp.bfloat16)
    combine_left = combine_mat.T
    mixed_blocks = []
    for group_index in range(block_count // group_size):
        out_block = expert_out[:, group_index * group_width : (group_index + 1) * group_width]
        returned_rows = lax.all_to_all(out_block, "node", split_axis=0, concat_axis=0, tiled=True)
        mixed_blocks.append(
            jnp.dot(
                combine_left, returned_rows.astype(jnp.float32), precision=lax.Precision.HIGHEST
            )
        )
    return jnp.concatenate(mixed_blocks, axis=1).astype(jnp.bfloat16)


def solution(mesh):
    in_specs = (
        P("node", "local"),
        P("local"),
        P("node", None),
        P("node", None),
        P("node", "local", None),
        P("node", "local", None),
        P("node", None, "local"),
    )
    out_specs = P("node", "local")
    return jax.shard_map(
        per_device, mesh=mesh, in_specs=in_specs, out_specs=out_specs, check_vma=False
    )
```

```python
import functools
import math

import jax
import jax.numpy as jnp
from jax import lax
from jax.experimental import pallas as pl
from jax.experimental.pallas import tpu as pltpu
from jax.sharding import PartitionSpec as P

HB = 128
LANES = 128
CHUNKS = 2
VMEM_BYTES = 63 * 1024 * 1024
MESH = pl.DeviceIdType.MESH


def fused_kernel(
    nodes,
    tok_hbm, sign_hbm, routes_hbm, gv_hbm, gw_hbm, uw_hbm, dw_hbm, out_ref,
    tok_ref, sign_ref, routes_ref, gv_ref, gw, uw, dw, arr,
    core_out, core_in, y_out, y_in, hid, acc, own, back_out, back_in,
    w_sem, ag_send, ag_recv, fw_send, core_send, core_recv, y_send, y_recv,
    hid_send, hid_recv, back_send, back_recv,
):
    rows, width = tok_hbm.shape
    nz = nodes // 2
    half = nz * rows
    piece = gw.shape[1] // 4
    cols = width // CHUNKS
    f32, bf16 = jnp.float32, jnp.bfloat16

    node = lax.axis_index("node")
    local = lax.axis_index("local")
    z, x = node // 2, node % 2
    y, c = local // 2, local % 2
    x_peer = {"node": z * 2 + (1 - x)}
    z_peers = [z + 1 - 2 * (z % 2), (z + 2) % nz, nz - 1 - z]
    core_peer_l, y_peer_l, far_l = y * 2 + (1 - c), (1 - y) * 2 + c, (1 - y) * 2 + (1 - c)
    core_peer, y_peer, far_peer = {"local": core_peer_l}, {"local": y_peer_l}, {"local": far_l}
    same_plane = [{"node": pz * 2 + x} for pz in z_peers]
    other_plane = [{"node": pz * 2 + (1 - x)} for pz in [z] + z_peers]

    barrier = pltpu.get_barrier_semaphore()
    peers = [core_peer, y_peer, x_peer] + same_plane
    for peer in peers:
        pl.semaphore_signal(barrier, inc=1, device_id=peer, device_id_type=MESH)

    loads = []
    for i, (src, dst) in enumerate((
        (tok_hbm, tok_ref), (sign_hbm, sign_ref), (routes_hbm, routes_ref), (gv_hbm, gv_ref),
        (gw_hbm.at[0], gw), (uw_hbm.at[0], uw), (dw_hbm.at[0], dw),
    )):
        load = pltpu.make_async_copy(src, dst, w_sem.at[i])
        load.start()
        loads.append(load)

    row_id = lax.broadcasted_iota(jnp.int32, (HB, HB), 0)
    col_id = lax.broadcasted_iota(jnp.int32, (HB, HB), 1)
    bits = row_id & col_id
    bits = bits ^ (bits >> 4)
    bits = bits ^ (bits >> 2)
    bits = bits ^ (bits >> 1)
    table = (1 - 2 * (bits & 1)).astype(f32).astype(bf16)
    for load in loads[:4]:
        load.wait()
    signs = (1 - 2 * sign_ref[...]).astype(f32)
    signed = (tok_ref[...].astype(f32) * signs).astype(bf16)
    for b in range(width // HB):
        block = jnp.dot(signed[:, b * HB : (b + 1) * HB], table, preferred_element_type=f32)
        arr[x, z, :, b * HB : (b + 1) * HB] = (block * (1.0 / math.sqrt(HB))).astype(bf16)
    code = lax.broadcasted_iota(jnp.int32, (LANES, rows), 0)
    dense = jnp.zeros((LANES, rows), f32)
    for k in range(routes_ref.shape[0]):
        hit = (code % nodes) == routes_ref[k : k + 1, :]
        dense = dense + jnp.where(hit, gv_ref[k : k + 1, :], 0.0)
    high = dense.astype(bf16).astype(f32)
    middle = (dense - high).astype(bf16).astype(f32)
    low = dense - high - middle
    parts = jnp.where(code < nodes, high, jnp.where(code < 2 * nodes, middle, low))
    parts = jnp.where(code < 3 * nodes, parts, 0.0).astype(bf16)
    same = lax.broadcasted_iota(jnp.int32, (rows, rows), 0) == lax.broadcasted_iota(jnp.int32, (rows, rows), 1)
    turned = lax.dot_general(
        same.astype(f32).astype(bf16), parts, (((1,), (1,)), ((), ())), preferred_element_type=f32
    )
    arr[x, z, :, width:] = turned.astype(bf16)

    pl.semaphore_wait(barrier, len(peers))

    def gather(plane, pz, send_sem, peer):
        return pltpu.make_async_remote_copy(
            src_ref=arr.at[plane, pz], dst_ref=arr.at[plane, pz], send_sem=send_sem,
            recv_sem=ag_recv.at[plane, pz], device_id=peer, device_id_type=MESH,
        )

    sent = []

    def start(copy):
        copy.start()
        sent.append(copy)
        return copy

    def push(src, dst, send_sem, recv_sem, peer):
        return start(pltpu.make_async_remote_copy(
            src_ref=src, dst_ref=dst, send_sem=send_sem, recv_sem=recv_sem,
            device_id=peer, device_id_type=MESH,
        ))

    for i in (1, 2, 0):
        start(gather(x, z, ag_send.at[i], same_plane[i]))
    start(gather(x, z, fw_send.at[nz - 1], x_peer))
    for i, pz in enumerate(z_peers):
        copy = gather(x, pz, fw_send.at[i], x_peer)
        copy.wait_recv()
        start(copy)
    loads[4].wait()
    loads[5].wait()

    planes = (x, 1 - x)

    def partial_sums(group, p):
        where = pl.ds(pl.multiple_of(p * piece, piece), piece)
        tokens = arr[planes[group], :, :, :width].reshape(half, width)
        gate = jnp.dot(tokens, gw[:, where], preferred_element_type=f32)
        up = jnp.dot(tokens, uw[:, where], preferred_element_type=f32)
        return gate, up

    def to_core(i, group, p):
        gate, up = partial_sums(group, p)
        core_out[i, :, :piece] = gate.astype(bf16)
        core_out[i, :, piece:] = up.astype(bf16)
        return push(core_out.at[i], core_in.at[i], core_send.at[i], core_recv.at[i], core_peer)

    def add_core(i, copy, gate, up):
        copy.wait_recv()
        return gate + core_in[i, :, :piece].astype(f32), up + core_in[i, :, piece:].astype(f32)

    def to_y(group):
        copy = to_core(group, group, far_l)
        gate, up = add_core(group, copy, *partial_sums(group, y_peer_l))
        y_out[group, :, :piece] = gate.astype(bf16)
        y_out[group, :, piece:] = up.astype(bf16)
        return push(y_out.at[group], y_in.at[group], y_send.at[group], y_recv.at[group], y_peer)

    def spread(group, p, i, peer):
        return pltpu.make_async_remote_copy(
            src_ref=hid.at[group, p], dst_ref=hid.at[group, p], send_sem=hid_send.at[group, i],
            recv_sem=hid_recv.at[group, p], device_id=peer, device_id_type=MESH,
        )

    def activate(group, gate, up, over_y):
        over_y.wait_recv()
        gate = gate + y_in[group, :, :piece].astype(f32)
        up = up + y_in[group, :, piece:].astype(f32)
        hid[group, local] = (gate / (1.0 + jnp.exp(-gate)) * up).astype(bf16)
        for i, peer in enumerate((y_peer, far_peer, core_peer)):
            start(spread(group, local, i, peer))

    over_y0 = to_y(0)
    near0 = to_core(2, 0, core_peer_l)
    for pz in [z] + z_peers:
        gather(1 - x, pz, fw_send.at[0], x_peer).wait_recv()
    over_y1 = to_y(1)
    gate0, up0 = partial_sums(0, local)
    near1 = to_core(3, 1, core_peer_l)
    activate(0, *add_core(2, near0, gate0, up0), over_y0)
    gate1, up1 = partial_sums(1, local)
    activate(1, *add_core(3, near1, gate1, up1), over_y1)
    loads[6].wait()

    chunk_at = [slice(j * cols, (j + 1) * cols) for j in range(CHUNKS)]

    def down(group, p, where):
        depth = pl.ds(pl.multiple_of(p * piece, piece), piece)
        return jnp.dot(hid[group, p], dw[depth, where], preferred_element_type=f32)

    lane = lax.broadcasted_iota(jnp.int32, (half, LANES), 1)
    mine = (lane == node) | (lane == node + nodes) | (lane == node + 2 * nodes)

    def give_back(group):
        for where in chunk_at:
            acc[group, :, where] = down(group, local, where)
        for p in (core_peer_l, y_peer_l):
            spread(group, p, 0, core_peer).wait_recv()
            for where in chunk_at:
                acc[group, :, where] += down(group, p, where)
        coded = arr[planes[group], :, :, width:].reshape(half, LANES).astype(f32)
        weight = jnp.sum(jnp.where(mine, coded, 0.0), axis=1, keepdims=True)
        spread(group, far_l, 0, core_peer).wait_recv()
        targets = ([z] + z_peers, other_plane) if group else (z_peers, same_plane)
        for j, where in enumerate(chunk_at):
            result = (acc[group, :, where] + down(group, far_l, where)).astype(bf16).astype(f32)
            weighted = (result * weight).reshape(nz, rows, cols)
            back_out[group, j] = weighted.astype(bf16)
            if group == 0:
                own[j] = weighted
            for i, (pz, peer) in enumerate(zip(*targets)):
                slot = i + group * (nz - 1)
                push(back_out.at[group, j, pz], back_in.at[j, slot],
                     back_send.at[j, slot], back_recv.at[j, slot], peer)

    give_back(0)
    give_back(1)
    for copy in sent:
        copy.wait_send()

    for j, where in enumerate(chunk_at):
        mixed = own[j, z]
        for i in range(nodes - 1):
            pltpu.make_async_remote_copy(
                src_ref=back_out.at[0, j, 0], dst_ref=back_in.at[j, i], send_sem=back_send.at[j, i],
                recv_sem=back_recv.at[j, i], device_id=x_peer, device_id_type=MESH,
            ).wait_recv()
            mixed = mixed + back_in[j, i].astype(f32)
        out_ref[:, where] = mixed.astype(bf16)


def fused(tokens, sign_bits, routes, gate_values, gate_w, up_w, down_w):
    nodes = lax.axis_size("node")
    rows, width = tokens.shape
    hidden = gate_w.shape[2]
    nz, piece, cols = nodes // 2, hidden // 4, width // CHUNKS
    total, half = nodes * rows, nz * rows
    bf16, f32 = jnp.bfloat16, jnp.float32
    dma = pltpu.SemaphoreType.DMA
    vmem = pl.BlockSpec(memory_space=pltpu.VMEM)
    hbm = pl.BlockSpec(memory_space=pltpu.HBM)
    return pl.pallas_call(
        functools.partial(fused_kernel, nodes),
        out_shape=pltpu.VMEM((rows, width), bf16),
        in_specs=[hbm] * 7,
        out_specs=vmem,
        scratch_shapes=[
            pltpu.VMEM((rows, width), bf16),
            pltpu.VMEM((1, width), jnp.int32),
            pltpu.VMEM((routes.shape[1], rows), jnp.int32),
            pltpu.VMEM((routes.shape[1], rows), f32),
            pltpu.VMEM((width, hidden), bf16),
            pltpu.VMEM((width, hidden), bf16),
            pltpu.VMEM((hidden, width), bf16),
            pltpu.VMEM((2, nz, rows, width + LANES), bf16),
            pltpu.VMEM((4, half, 2 * piece), bf16),
            pltpu.VMEM((4, half, 2 * piece), bf16),
            pltpu.VMEM((2, half, 2 * piece), bf16),
            pltpu.VMEM((2, half, 2 * piece), bf16),
            pltpu.VMEM((2, 4, half, piece), bf16),
            pltpu.VMEM((2, half, width), f32),
            pltpu.VMEM((CHUNKS, nz, rows, cols), f32),
            pltpu.VMEM((2, CHUNKS, nz, rows, cols), bf16),
            pltpu.VMEM((CHUNKS, nodes - 1, rows, cols), bf16),
            dma((7,)),
            dma((nz - 1,)), dma((2, nz)), dma((nz,)),
            dma((4,)), dma((4,)), dma((2,)), dma((2,)),
            dma((2, 3)), dma((2, 4)),
            dma((CHUNKS, nodes - 1)), dma((CHUNKS, nodes - 1)),
        ],
        compiler_params=pltpu.CompilerParams(
            collective_id=0, has_side_effects=True, vmem_limit_bytes=VMEM_BYTES
        ),
        cost_estimate=pl.CostEstimate(
            flops=6 * total * width * hidden, bytes_accessed=6 * width * hidden, transcendentals=0
        ),
    )(tokens, sign_bits.reshape(1, width), routes.T, gate_values.T, gate_w, up_w, down_w)


def fits_fused(tokens, routes, gate_w, capacity):
    nodes, rows = lax.axis_size("node"), tokens.shape[0]
    return (
        capacity >= rows
        and nodes == 8
        and lax.axis_size("local") == 4
        and rows % 16 == 0
        and nodes * rows <= 256
        and tokens.shape[1] % (CHUNKS * LANES) == 0
        and gate_w.shape[2] % (4 * LANES) == 0
    )


def hadamard_table(block_order):
    kernel_two = jnp.array([[1.0, 1.0], [1.0, -1.0]], jnp.float32)
    matrix = jnp.ones((1, 1), jnp.float32)
    while matrix.shape[0] < block_order:
        matrix = jnp.kron(matrix, kernel_two)
    return matrix / math.sqrt(block_order)


def slot_table(routes, experts, capacity):
    rows_all = routes.shape[0] * routes.shape[1]
    flat_routes = routes.reshape(rows_all)
    onehot = (flat_routes[:, None] == jnp.arange(experts, dtype=jnp.int32)[None, :]).astype(
        jnp.int32
    )
    ranks = jnp.sum(jnp.cumsum(onehot, axis=0) * onehot, axis=1) - 1
    slot_ids = flat_routes * capacity + ranks
    return slot_ids[None, :] == jnp.arange(experts * capacity, dtype=jnp.int32)[:, None]


def per_device(tokens, sign_bits, routes, gate_values, gate_w, up_w, down_w):
    experts = lax.axis_size("node")
    tok_node, width_dev = tokens.shape
    top_count = routes.shape[1]
    capacity = max(2, 2 * tok_node * top_count // experts)
    if fits_fused(tokens, routes, gate_w, capacity):
        return fused(tokens, sign_bits, routes, gate_values, gate_w, up_w, down_w)
    placed = slot_table(routes, experts, capacity).reshape(experts * capacity, tok_node, top_count)
    scatter_mat = jnp.any(placed, axis=2).astype(jnp.bfloat16)
    combine_mat = jnp.sum(placed.astype(jnp.float32) * gate_values[None, :, :], axis=2)
    hadamard = hadamard_table(HB)
    sign_vals = (1 - 2 * sign_bits).astype(jnp.float32)
    signed = tokens.astype(jnp.float32) * sign_vals[None, :]
    block_count = width_dev // HB
    group_size = min(2, block_count)
    group_width = group_size * HB
    received = []
    for group_index in range(block_count // group_size):
        rotated_parts = []
        for inner_index in range(group_size):
            first_col = group_index * group_width + inner_index * HB
            feature_block = signed[:, first_col : first_col + HB]
            rotated_parts.append(
                jnp.dot(feature_block, hadamard, precision=lax.Precision.HIGHEST).astype(
                    jnp.bfloat16
                )
            )
        rotated = jnp.concatenate(rotated_parts, axis=1)
        outgoing = jnp.dot(scatter_mat, rotated, preferred_element_type=jnp.float32).astype(
            jnp.bfloat16
        )
        received.append(lax.all_to_all(outgoing, "node", split_axis=0, concat_axis=0, tiled=True))
    arrived = jnp.concatenate(received, axis=1)
    gate_part = jnp.dot(arrived, gate_w[0], preferred_element_type=jnp.float32)
    up_part = jnp.dot(arrived, up_w[0], preferred_element_type=jnp.float32)
    gate_full, up_full = lax.psum((gate_part, up_part), "local")
    hidden_full = (jax.nn.silu(gate_full) * up_full).astype(jnp.bfloat16)
    expert_sum = jnp.dot(hidden_full, down_w[0], preferred_element_type=jnp.float32)
    expert_out = expert_sum.astype(jnp.bfloat16)
    combine_left = combine_mat.T
    mixed_blocks = []
    for group_index in range(block_count // group_size):
        out_block = expert_out[:, group_index * group_width : (group_index + 1) * group_width]
        returned_rows = lax.all_to_all(out_block, "node", split_axis=0, concat_axis=0, tiled=True)
        mixed_blocks.append(
            jnp.dot(
                combine_left, returned_rows.astype(jnp.float32), precision=lax.Precision.HIGHEST
            )
        )
    return jnp.concatenate(mixed_blocks, axis=1).astype(jnp.bfloat16)


def solution(mesh):
    in_specs = (
        P("node", "local"),
        P("local"),
        P("node", None),
        P("node", None),
        P("node", "local", None),
        P("node", "local", None),
        P("node", None, "local"),
    )
    out_specs = P("node", "local")
    return jax.shard_map(
        per_device, mesh=mesh, in_specs=in_specs, out_specs=out_specs, check_vma=False
    )
```

```python
import functools
import math

import jax
import jax.numpy as jnp
from jax import lax
from jax.experimental import pallas as pl
from jax.experimental.pallas import tpu as pltpu
from jax.sharding import PartitionSpec as P

HB = 128
LANES = 128
CHUNKS = 2
VMEM_BYTES = 63 * 1024 * 1024
MESH = pl.DeviceIdType.MESH


def fused_kernel(
    nodes,
    tok_hbm, sign_hbm, routes_hbm, gv_hbm, gw_hbm, uw_hbm, dw_hbm, out_ref,
    tok_ref, sign_ref, routes_ref, gv_ref, gw, uw, dw, arr, gates,
    core_out, core_in, y_out, y_in, hid, acc, own, back_out, back_in,
    w_sem, ag_send, ag_recv, fw_send, gate_send, gate_recv, core_send, core_recv, y_send, y_recv,
    hid_send, hid_recv, back_send, back_recv,
):
    rows, width = tok_hbm.shape
    nz = nodes // 2
    half = nz * rows
    piece = gw.shape[1] // 4
    cols = width // CHUNKS
    f32, bf16 = jnp.float32, jnp.bfloat16

    node = lax.axis_index("node")
    local = lax.axis_index("local")
    z, x = node // 2, node % 2
    y, c = local // 2, local % 2
    x_peer = {"node": z * 2 + (1 - x)}
    z_peers = [z + 1 - 2 * (z % 2), (z + 2) % nz, nz - 1 - z]
    core_peer_l, y_peer_l, far_l = y * 2 + (1 - c), (1 - y) * 2 + c, (1 - y) * 2 + (1 - c)
    core_peer, y_peer, far_peer = {"local": core_peer_l}, {"local": y_peer_l}, {"local": far_l}
    same_plane = [{"node": pz * 2 + x} for pz in z_peers]
    other_plane = [{"node": pz * 2 + (1 - x)} for pz in [z] + z_peers]

    barrier = pltpu.get_barrier_semaphore()
    peers = [core_peer, y_peer, x_peer] + same_plane
    for peer in peers:
        pl.semaphore_signal(barrier, inc=1, device_id=peer, device_id_type=MESH)

    loads = []
    for i, (src, dst) in enumerate((
        (tok_hbm, tok_ref), (sign_hbm, sign_ref), (routes_hbm, routes_ref), (gv_hbm, gv_ref),
        (gw_hbm.at[0], gw), (uw_hbm.at[0], uw), (dw_hbm.at[0], dw),
    )):
        load = pltpu.make_async_copy(src, dst, w_sem.at[i])
        load.start()
        loads.append(load)

    row_id = lax.broadcasted_iota(jnp.int32, (HB, HB), 0)
    col_id = lax.broadcasted_iota(jnp.int32, (HB, HB), 1)
    bits = row_id & col_id
    bits = bits ^ (bits >> 4)
    bits = bits ^ (bits >> 2)
    bits = bits ^ (bits >> 1)
    table = (1 - 2 * (bits & 1)).astype(f32).astype(bf16)
    loads[0].wait()
    loads[1].wait()
    signs = (1 - 2 * sign_ref[...]).astype(f32)
    signed = (tok_ref[...].astype(f32) * signs).astype(bf16)
    count = width // HB
    stacked = jnp.concatenate([signed[:, b * HB : (b + 1) * HB] for b in range(count)], axis=0)
    turned = jnp.dot(stacked, table, preferred_element_type=f32) * (1.0 / math.sqrt(HB))
    for b in range(count):
        arr[x, z, :, b * HB : (b + 1) * HB] = turned[b * rows : (b + 1) * rows].astype(bf16)

    pl.semaphore_wait(barrier, len(peers))

    def gather(plane, pz, send_sem, peer):
        return pltpu.make_async_remote_copy(
            src_ref=arr.at[plane, pz], dst_ref=arr.at[plane, pz], send_sem=send_sem,
            recv_sem=ag_recv.at[plane, pz], device_id=peer, device_id_type=MESH,
        )

    sent = []

    def start(copy):
        copy.start()
        sent.append(copy)
        return copy

    def push(src, dst, send_sem, recv_sem, peer):
        return start(pltpu.make_async_remote_copy(
            src_ref=src, dst_ref=dst, send_sem=send_sem, recv_sem=recv_sem,
            device_id=peer, device_id_type=MESH,
        ))

    for i in (1, 2, 0):
        start(gather(x, z, ag_send.at[i], same_plane[i]))
    start(gather(x, z, fw_send.at[nz - 1], x_peer))
    for i, pz in enumerate(z_peers):
        copy = gather(x, pz, fw_send.at[i], x_peer)
        copy.wait_recv()
        start(copy)
    loads[4].wait()
    loads[5].wait()

    planes = (x, 1 - x)

    def partial_sums(group, p):
        where = pl.ds(pl.multiple_of(p * piece, piece), piece)
        tokens = arr[planes[group]].reshape(half, width)
        gate = jnp.dot(tokens, gw[:, where], preferred_element_type=f32)
        up = jnp.dot(tokens, uw[:, where], preferred_element_type=f32)
        return gate, up

    def to_core(i, group, p):
        gate, up = partial_sums(group, p)
        core_out[i, :, :piece] = gate.astype(bf16)
        core_out[i, :, piece:] = up.astype(bf16)
        return push(core_out.at[i], core_in.at[i], core_send.at[i], core_recv.at[i], core_peer)

    def add_core(i, copy, gate, up):
        copy.wait_recv()
        return gate + core_in[i, :, :piece].astype(f32), up + core_in[i, :, piece:].astype(f32)

    def to_y(group):
        copy = to_core(group, group, far_l)
        gate, up = add_core(group, copy, *partial_sums(group, y_peer_l))
        y_out[group, :, :piece] = gate.astype(bf16)
        y_out[group, :, piece:] = up.astype(bf16)
        return push(y_out.at[group], y_in.at[group], y_send.at[group], y_recv.at[group], y_peer)

    def spread(group, p, i, peer):
        return pltpu.make_async_remote_copy(
            src_ref=hid.at[group, p], dst_ref=hid.at[group, p], send_sem=hid_send.at[group, i],
            recv_sem=hid_recv.at[group, p], device_id=peer, device_id_type=MESH,
        )

    def activate(group, gate, up, over_y):
        over_y.wait_recv()
        gate = gate + y_in[group, :, :piece].astype(f32)
        up = up + y_in[group, :, piece:].astype(f32)
        hid[group, local] = (gate / (1.0 + jnp.exp(-gate)) * up).astype(bf16)
        for i, peer in enumerate((y_peer, far_peer, core_peer)):
            start(spread(group, local, i, peer))

    over_y0 = to_y(0)
    near0 = to_core(2, 0, core_peer_l)
    for pz in [z] + z_peers:
        gather(1 - x, pz, fw_send.at[0], x_peer).wait_recv()
    over_y1 = to_y(1)
    gate0, up0 = partial_sums(0, local)

    loads[2].wait()
    loads[3].wait()
    code = lax.broadcasted_iota(jnp.int32, (LANES, rows), 0)
    dense = jnp.zeros((LANES, rows), f32)
    for k in range(routes_ref.shape[0]):
        hit = (code % nodes) == routes_ref[k : k + 1, :]
        dense = dense + jnp.where(hit, gv_ref[k : k + 1, :], 0.0)
    high = dense.astype(bf16).astype(f32)
    middle = (dense - high).astype(bf16).astype(f32)
    low = dense - high - middle
    parts = jnp.where(code < nodes, high, jnp.where(code < 2 * nodes, middle, low))
    parts = jnp.where(code < 3 * nodes, parts, 0.0).astype(bf16)
    same = lax.broadcasted_iota(jnp.int32, (rows, rows), 0) == lax.broadcasted_iota(jnp.int32, (rows, rows), 1)
    turned = lax.dot_general(
        same.astype(f32).astype(bf16), parts, (((1,), (1,)), ((), ())), preferred_element_type=f32
    )
    gates[x, z] = turned.astype(bf16)
    for i, peer in enumerate(same_plane + other_plane):
        push(gates.at[x, z], gates.at[x, z], gate_send.at[i], gate_recv.at[x, z], peer)

    activate(0, *add_core(2, near0, gate0, up0), over_y0)
    near1 = to_core(3, 1, core_peer_l)
    gate1, up1 = partial_sums(1, local)
    activate(1, *add_core(3, near1, gate1, up1), over_y1)
    loads[6].wait()

    chunk_at = [slice(j * cols, (j + 1) * cols) for j in range(CHUNKS)]

    def down(group, p, where):
        depth = pl.ds(pl.multiple_of(p * piece, piece), piece)
        return jnp.dot(hid[group, p], dw[depth, where], preferred_element_type=f32)

    lane = lax.broadcasted_iota(jnp.int32, (half, LANES), 1)
    mine = (lane == node) | (lane == node + nodes) | (lane == node + 2 * nodes)

    def give_back(group):
        for where in chunk_at:
            acc[group, :, where] = down(group, local, where)
        for p in (core_peer_l, y_peer_l):
            spread(group, p, 0, core_peer).wait_recv()
            for where in chunk_at:
                acc[group, :, where] += down(group, p, where)
        for pz in z_peers + ([z] if group else []):
            pltpu.make_async_remote_copy(
                src_ref=gates.at[x, z], dst_ref=gates.at[planes[group], pz], send_sem=gate_send.at[0],
                recv_sem=gate_recv.at[planes[group], pz], device_id=x_peer, device_id_type=MESH,
            ).wait_recv()
        coded = gates[planes[group]].reshape(half, LANES).astype(f32)
        weight = jnp.sum(jnp.where(mine, coded, 0.0), axis=1, keepdims=True)
        spread(group, far_l, 0, core_peer).wait_recv()
        targets = ([z] + z_peers, other_plane) if group else (z_peers, same_plane)
        for j, where in enumerate(chunk_at):
            result = (acc[group, :, where] + down(group, far_l, where)).astype(bf16).astype(f32)
            weighted = (result * weight).reshape(nz, rows, cols)
            back_out[group, j] = weighted.astype(bf16)
            if group == 0:
                own[j] = weighted
            for i in ((2, 3, 1, 0) if group else (1, 2, 0)):
                pz, peer = targets[0][i], targets[1][i]
                slot = i + group * (nz - 1)
                push(back_out.at[group, j, pz], back_in.at[j, slot],
                     back_send.at[j, slot], back_recv.at[j, slot], peer)

    give_back(0)
    give_back(1)
    for copy in sent:
        copy.wait_send()

    for j, where in enumerate(chunk_at):
        mixed = own[j, z]
        for i in range(nodes - 1):
            pltpu.make_async_remote_copy(
                src_ref=back_out.at[0, j, 0], dst_ref=back_in.at[j, i], send_sem=back_send.at[j, i],
                recv_sem=back_recv.at[j, i], device_id=x_peer, device_id_type=MESH,
            ).wait_recv()
            mixed = mixed + back_in[j, i].astype(f32)
        out_ref[:, where] = mixed.astype(bf16)


def fused(tokens, sign_bits, routes, gate_values, gate_w, up_w, down_w):
    nodes = lax.axis_size("node")
    rows, width = tokens.shape
    hidden = gate_w.shape[2]
    nz, piece, cols = nodes // 2, hidden // 4, width // CHUNKS
    total, half = nodes * rows, nz * rows
    bf16, f32 = jnp.bfloat16, jnp.float32
    dma = pltpu.SemaphoreType.DMA
    vmem = pl.BlockSpec(memory_space=pltpu.VMEM)
    hbm = pl.BlockSpec(memory_space=pltpu.HBM)
    return pl.pallas_call(
        functools.partial(fused_kernel, nodes),
        out_shape=pltpu.VMEM((rows, width), bf16),
        in_specs=[hbm] * 7,
        out_specs=vmem,
        scratch_shapes=[
            pltpu.VMEM((rows, width), bf16),
            pltpu.VMEM((1, width), jnp.int32),
            pltpu.VMEM((routes.shape[1], rows), jnp.int32),
            pltpu.VMEM((routes.shape[1], rows), f32),
            pltpu.VMEM((width, hidden), bf16),
            pltpu.VMEM((width, hidden), bf16),
            pltpu.VMEM((hidden, width), bf16),
            pltpu.VMEM((2, nz, rows, width), bf16),
            pltpu.VMEM((2, nz, rows, LANES), bf16),
            pltpu.VMEM((4, half, 2 * piece), bf16),
            pltpu.VMEM((4, half, 2 * piece), bf16),
            pltpu.VMEM((2, half, 2 * piece), bf16),
            pltpu.VMEM((2, half, 2 * piece), bf16),
            pltpu.VMEM((2, 4, half, piece), bf16),
            pltpu.VMEM((2, half, width), f32),
            pltpu.VMEM((CHUNKS, nz, rows, cols), f32),
            pltpu.VMEM((2, CHUNKS, nz, rows, cols), bf16),
            pltpu.VMEM((CHUNKS, nodes - 1, rows, cols), bf16),
            dma((7,)),
            dma((nz - 1,)), dma((2, nz)), dma((nz,)), dma((nodes - 1,)), dma((2, nz)),
            dma((4,)), dma((4,)), dma((2,)), dma((2,)),
            dma((2, 3)), dma((2, 4)),
            dma((CHUNKS, nodes - 1)), dma((CHUNKS, nodes - 1)),
        ],
        compiler_params=pltpu.CompilerParams(
            collective_id=0, has_side_effects=True, vmem_limit_bytes=VMEM_BYTES
        ),
        cost_estimate=pl.CostEstimate(
            flops=6 * total * width * hidden, bytes_accessed=6 * width * hidden, transcendentals=0
        ),
    )(tokens, sign_bits.reshape(1, width), routes.T, gate_values.T, gate_w, up_w, down_w)


def fits_fused(tokens, routes, gate_w, capacity):
    nodes, rows = lax.axis_size("node"), tokens.shape[0]
    return (
        capacity >= rows
        and nodes == 8
        and lax.axis_size("local") == 4
        and rows % 16 == 0
        and nodes * rows <= 256
        and tokens.shape[1] % (CHUNKS * LANES) == 0
        and gate_w.shape[2] % (4 * LANES) == 0
    )


def hadamard_table(block_order):
    kernel_two = jnp.array([[1.0, 1.0], [1.0, -1.0]], jnp.float32)
    matrix = jnp.ones((1, 1), jnp.float32)
    while matrix.shape[0] < block_order:
        matrix = jnp.kron(matrix, kernel_two)
    return matrix / math.sqrt(block_order)


def slot_table(routes, experts, capacity):
    rows_all = routes.shape[0] * routes.shape[1]
    flat_routes = routes.reshape(rows_all)
    onehot = (flat_routes[:, None] == jnp.arange(experts, dtype=jnp.int32)[None, :]).astype(
        jnp.int32
    )
    ranks = jnp.sum(jnp.cumsum(onehot, axis=0) * onehot, axis=1) - 1
    slot_ids = flat_routes * capacity + ranks
    return slot_ids[None, :] == jnp.arange(experts * capacity, dtype=jnp.int32)[:, None]


def per_device(tokens, sign_bits, routes, gate_values, gate_w, up_w, down_w):
    experts = lax.axis_size("node")
    tok_node, width_dev = tokens.shape
    top_count = routes.shape[1]
    capacity = max(2, 2 * tok_node * top_count // experts)
    if fits_fused(tokens, routes, gate_w, capacity):
        return fused(tokens, sign_bits, routes, gate_values, gate_w, up_w, down_w)
    placed = slot_table(routes, experts, capacity).reshape(experts * capacity, tok_node, top_count)
    scatter_mat = jnp.any(placed, axis=2).astype(jnp.bfloat16)
    combine_mat = jnp.sum(placed.astype(jnp.float32) * gate_values[None, :, :], axis=2)
    hadamard = hadamard_table(HB)
    sign_vals = (1 - 2 * sign_bits).astype(jnp.float32)
    signed = tokens.astype(jnp.float32) * sign_vals[None, :]
    block_count = width_dev // HB
    group_size = min(2, block_count)
    group_width = group_size * HB
    received = []
    for group_index in range(block_count // group_size):
        rotated_parts = []
        for inner_index in range(group_size):
            first_col = group_index * group_width + inner_index * HB
            feature_block = signed[:, first_col : first_col + HB]
            rotated_parts.append(
                jnp.dot(feature_block, hadamard, precision=lax.Precision.HIGHEST).astype(
                    jnp.bfloat16
                )
            )
        rotated = jnp.concatenate(rotated_parts, axis=1)
        outgoing = jnp.dot(scatter_mat, rotated, preferred_element_type=jnp.float32).astype(
            jnp.bfloat16
        )
        received.append(lax.all_to_all(outgoing, "node", split_axis=0, concat_axis=0, tiled=True))
    arrived = jnp.concatenate(received, axis=1)
    gate_part = jnp.dot(arrived, gate_w[0], preferred_element_type=jnp.float32)
    up_part = jnp.dot(arrived, up_w[0], preferred_element_type=jnp.float32)
    gate_full, up_full = lax.psum((gate_part, up_part), "local")
    hidden_full = (jax.nn.silu(gate_full) * up_full).astype(jnp.bfloat16)
    expert_sum = jnp.dot(hidden_full, down_w[0], preferred_element_type=jnp.float32)
    expert_out = expert_sum.astype(jnp.bfloat16)
    combine_left = combine_mat.T
    mixed_blocks = []
    for group_index in range(block_count // group_size):
        out_block = expert_out[:, group_index * group_width : (group_index + 1) * group_width]
        returned_rows = lax.all_to_all(out_block, "node", split_axis=0, concat_axis=0, tiled=True)
        mixed_blocks.append(
            jnp.dot(
                combine_left, returned_rows.astype(jnp.float32), precision=lax.Precision.HIGHEST
            )
        )
    return jnp.concatenate(mixed_blocks, axis=1).astype(jnp.bfloat16)


def solution(mesh):
    in_specs = (
        P("node", "local"),
        P("local"),
        P("node", None),
        P("node", None),
        P("node", "local", None),
        P("node", "local", None),
        P("node", None, "local"),
    )
    out_specs = P("node", "local")
    return jax.shard_map(
        per_device, mesh=mesh, in_specs=in_specs, out_specs=out_specs, check_vma=False
    )
```

```python
import functools
import math

import jax
import jax.numpy as jnp
from jax import lax
from jax.experimental import pallas as pl
from jax.experimental.pallas import tpu as pltpu
from jax.sharding import PartitionSpec as P

HB = 128
LANES = 128
CHUNKS = 1
VMEM_BYTES = 63 * 1024 * 1024
MESH = pl.DeviceIdType.MESH


def fused_kernel(
    nodes,
    tok_hbm, sign_hbm, routes_hbm, gv_hbm, gw_hbm, uw_hbm, dw_hbm, out_ref,
    tok_ref, sign_ref, routes_ref, gv_ref, gw, uw, dw, arr, gates,
    core_out, core_in, y_out, y_in, hid, acc, own, back_out, back_in,
    w_sem, ag_send, ag_recv, fw_send, gate_send, gate_recv, core_send, core_recv, y_send, y_recv,
    hid_send, hid_recv, back_send, back_recv,
):
    rows, width = tok_hbm.shape
    nz = nodes // 2
    part = 2 * rows
    piece = gw.shape[1] // 4
    cols = width // CHUNKS
    f32, bf16 = jnp.float32, jnp.bfloat16

    node = lax.axis_index("node")
    local = lax.axis_index("local")
    z, x = node // 2, node % 2
    y, c = local // 2, local % 2
    x_peer = {"node": z * 2 + (1 - x)}
    z_peers = [z + 1 - 2 * (z % 2), (z + 2) % nz, nz - 1 - z]
    core_peer_l, y_peer_l, far_l = y * 2 + (1 - c), (1 - y) * 2 + c, (1 - y) * 2 + (1 - c)
    core_peer, y_peer, far_peer = {"local": core_peer_l}, {"local": y_peer_l}, {"local": far_l}
    same_plane = [{"node": pz * 2 + x} for pz in z_peers]
    other_plane = [{"node": pz * 2 + (1 - x)} for pz in [z] + z_peers]

    barrier = pltpu.get_barrier_semaphore()
    peers = [core_peer, y_peer, x_peer] + same_plane
    for peer in peers:
        pl.semaphore_signal(barrier, inc=1, device_id=peer, device_id_type=MESH)

    loads = []
    for i, (src, dst) in enumerate((
        (tok_hbm, tok_ref), (sign_hbm, sign_ref), (routes_hbm, routes_ref), (gv_hbm, gv_ref),
        (gw_hbm.at[0], gw), (uw_hbm.at[0], uw), (dw_hbm.at[0], dw),
    )):
        load = pltpu.make_async_copy(src, dst, w_sem.at[i])
        load.start()
        loads.append(load)

    row_id = lax.broadcasted_iota(jnp.int32, (HB, HB), 0)
    col_id = lax.broadcasted_iota(jnp.int32, (HB, HB), 1)
    bits = row_id & col_id
    bits = bits ^ (bits >> 4)
    bits = bits ^ (bits >> 2)
    bits = bits ^ (bits >> 1)
    table = (1 - 2 * (bits & 1)).astype(f32).astype(bf16)
    loads[0].wait()
    loads[1].wait()
    signs = (1 - 2 * sign_ref[...]).astype(f32)
    signed = (tok_ref[...].astype(f32) * signs).astype(bf16)
    count = width // HB
    stacked = jnp.concatenate([signed[:, b * HB : (b + 1) * HB] for b in range(count)], axis=0)
    turned = jnp.dot(stacked, table, preferred_element_type=f32) * (1.0 / math.sqrt(HB))
    for b in range(count):
        arr[x, z // 2, z % 2, :, b * HB : (b + 1) * HB] = turned[b * rows : (b + 1) * rows].astype(bf16)

    pl.semaphore_wait(barrier, len(peers))

    def gather(plane, pz, send_sem, peer):
        return pltpu.make_async_remote_copy(
            src_ref=arr.at[plane, pz // 2, pz % 2], dst_ref=arr.at[plane, pz // 2, pz % 2], send_sem=send_sem,
            recv_sem=ag_recv.at[plane, pz], device_id=peer, device_id_type=MESH,
        )

    sent = []

    def start(copy):
        copy.start()
        sent.append(copy)
        return copy

    def push(src, dst, send_sem, recv_sem, peer):
        return start(pltpu.make_async_remote_copy(
            src_ref=src, dst_ref=dst, send_sem=send_sem, recv_sem=recv_sem,
            device_id=peer, device_id_type=MESH,
        ))

    for i in (1, 2, 0):
        start(gather(x, z, ag_send.at[i], same_plane[i]))
    start(gather(x, z, fw_send.at[nz - 1], x_peer))

    def relay(i):
        copy = gather(x, z_peers[i], fw_send.at[i], x_peer)
        copy.wait_recv()
        start(copy)

    near, far = z // 2, 1 - z // 2
    groups = ((x, near), (x, far), (1 - x, far), (1 - x, near))
    group_z = ((z, z_peers[0]), z_peers[1:], z_peers[1:], (z, z_peers[0]))

    def partial_sums(group, p):
        where = pl.ds(pl.multiple_of(p * piece, piece), piece)
        tokens = arr[groups[group]].reshape(part, width)
        gate = jnp.dot(tokens, gw[:, where], preferred_element_type=f32)
        up = jnp.dot(tokens, uw[:, where], preferred_element_type=f32)
        return gate, up

    def to_core(i, group, p):
        gate, up = partial_sums(group, p)
        core_out[i, :, :piece] = gate.astype(bf16)
        core_out[i, :, piece:] = up.astype(bf16)
        return push(core_out.at[i], core_in.at[i], core_send.at[i], core_recv.at[i], core_peer)

    def add_core(i, copy, gate, up):
        copy.wait_recv()
        return gate + core_in[i, :, :piece].astype(f32), up + core_in[i, :, piece:].astype(f32)

    def first_piece(group):
        copy = to_core(2 * group, group, far_l)
        return (2 * group, copy, *partial_sums(group, y_peer_l))

    def to_y(group, begun):
        gate, up = add_core(*begun)
        y_out[group, :, :piece] = gate.astype(bf16)
        y_out[group, :, piece:] = up.astype(bf16)
        return push(y_out.at[group], y_in.at[group], y_send.at[group], y_recv.at[group], y_peer)

    def own_piece(group):
        copy = to_core(2 * group + 1, group, core_peer_l)
        return (2 * group + 1, copy, *partial_sums(group, local))

    def spread(group, p, i, peer):
        return pltpu.make_async_remote_copy(
            src_ref=hid.at[group, p], dst_ref=hid.at[group, p], send_sem=hid_send.at[group, i],
            recv_sem=hid_recv.at[group, p], device_id=peer, device_id_type=MESH,
        )

    def activate(group, begun, over_y):
        gate, up = add_core(*begun)
        over_y.wait_recv()
        gate = gate + y_in[group, :, :piece].astype(f32)
        up = up + y_in[group, :, piece:].astype(f32)
        hid[group, local] = (gate / (1.0 + jnp.exp(-gate)) * up).astype(bf16)
        for i, peer in enumerate((y_peer, far_peer, core_peer)):
            start(spread(group, local, i, peer))

    relay(0)
    loads[4].wait()
    loads[5].wait()
    first0 = first_piece(0)
    relay(1)
    relay(2)
    over_y0 = to_y(0, first0)
    first1 = first_piece(1)
    own0 = own_piece(0)
    over_y1 = to_y(1, first1)
    for pz in group_z[2]:
        gather(1 - x, pz, fw_send.at[0], x_peer).wait_recv()
    first2 = first_piece(2)
    own1 = own_piece(1)
    over_y2 = to_y(2, first2)
    for pz in group_z[3]:
        gather(1 - x, pz, fw_send.at[0], x_peer).wait_recv()
    first3 = first_piece(3)
    activate(0, own0, over_y0)
    over_y3 = to_y(3, first3)
    own2 = own_piece(2)

    loads[2].wait()
    loads[3].wait()
    code = lax.broadcasted_iota(jnp.int32, (LANES, rows), 0)
    dense = jnp.zeros((LANES, rows), f32)
    for k in range(routes_ref.shape[0]):
        hit = (code % nodes) == routes_ref[k : k + 1, :]
        dense = dense + jnp.where(hit, gv_ref[k : k + 1, :], 0.0)
    high = dense.astype(bf16).astype(f32)
    middle = (dense - high).astype(bf16).astype(f32)
    low = dense - high - middle
    parts = jnp.where(code < nodes, high, jnp.where(code < 2 * nodes, middle, low))
    parts = jnp.where(code < 3 * nodes, parts, 0.0).astype(bf16)
    same = lax.broadcasted_iota(jnp.int32, (rows, rows), 0) == lax.broadcasted_iota(jnp.int32, (rows, rows), 1)
    turned = lax.dot_general(
        same.astype(f32).astype(bf16), parts, (((1,), (1,)), ((), ())), preferred_element_type=f32
    )
    gates[x, near, z % 2] = turned.astype(bf16)
    for i, peer in enumerate(same_plane + other_plane):
        push(gates.at[x, near, z % 2], gates.at[x, near, z % 2], gate_send.at[i], gate_recv.at[x, z], peer)

    activate(1, own1, over_y1)
    own3 = own_piece(3)
    activate(2, own2, over_y2)
    loads[6].wait()

    chunk_at = [slice(j * cols, (j + 1) * cols) for j in range(CHUNKS)]

    def down(group, p, where):
        depth = pl.ds(pl.multiple_of(p * piece, piece), piece)
        return jnp.dot(hid[group, p], dw[depth, where], preferred_element_type=f32)

    lane = lax.broadcasted_iota(jnp.int32, (part, LANES), 1)
    mine = (lane == node) | (lane == node + nodes) | (lane == node + 2 * nodes)

    def give_back(group):
        for where in chunk_at:
            acc[group, :, where] = down(group, local, where)
        for p in (core_peer_l, y_peer_l):
            spread(group, p, 0, core_peer).wait_recv()
            for where in chunk_at:
                acc[group, :, where] += down(group, p, where)
        plane, pair = groups[group]
        for pz in group_z[group][1 if group == 0 else 0 :]:
            pltpu.make_async_remote_copy(
                src_ref=gates.at[x, near, z % 2], dst_ref=gates.at[plane, pair, pz % 2], send_sem=gate_send.at[0],
                recv_sem=gate_recv.at[plane, pz], device_id=x_peer, device_id_type=MESH,
            ).wait_recv()
        coded = gates[plane, pair].reshape(part, LANES).astype(f32)
        weight = jnp.sum(jnp.where(mine, coded, 0.0), axis=1, keepdims=True)
        spread(group, far_l, 0, core_peer).wait_recv()
        for j, where in enumerate(chunk_at):
            result = (acc[group, :, where] + down(group, far_l, where)).astype(bf16).astype(f32)
            weighted = (result * weight).reshape(2, rows, cols)
            back_out[group, j] = weighted.astype(bf16)
            if group == 0:
                own[j] = weighted
            for slot in ((0,), (1, 2), (5, 6), (4, 3))[group]:
                pz, peer = ((z_peers + [z] + z_peers)[slot], (same_plane + other_plane)[slot])
                push(back_out.at[group, j, pz % 2], back_in.at[j, slot],
                     back_send.at[j, slot], back_recv.at[j, slot], peer)

    give_back(0)
    activate(3, own3, over_y3)
    give_back(1)
    give_back(2)
    give_back(3)
    for copy in sent:
        copy.wait_send()

    for j, where in enumerate(chunk_at):
        mixed = own[j, z % 2]
        for i in range(nodes - 1):
            pltpu.make_async_remote_copy(
                src_ref=back_out.at[0, j, 0], dst_ref=back_in.at[j, i], send_sem=back_send.at[j, i],
                recv_sem=back_recv.at[j, i], device_id=x_peer, device_id_type=MESH,
            ).wait_recv()
            mixed = mixed + back_in[j, i].astype(f32)
        out_ref[:, where] = mixed.astype(bf16)


def fused(tokens, sign_bits, routes, gate_values, gate_w, up_w, down_w):
    nodes = lax.axis_size("node")
    rows, width = tokens.shape
    hidden = gate_w.shape[2]
    nz, piece, cols = nodes // 2, hidden // 4, width // CHUNKS
    total, part = nodes * rows, 2 * rows
    bf16, f32 = jnp.bfloat16, jnp.float32
    dma = pltpu.SemaphoreType.DMA
    vmem = pl.BlockSpec(memory_space=pltpu.VMEM)
    hbm = pl.BlockSpec(memory_space=pltpu.HBM)
    return pl.pallas_call(
        functools.partial(fused_kernel, nodes),
        out_shape=pltpu.VMEM((rows, width), bf16),
        in_specs=[hbm] * 7,
        out_specs=vmem,
        scratch_shapes=[
            pltpu.VMEM((rows, width), bf16),
            pltpu.VMEM((1, width), jnp.int32),
            pltpu.VMEM((routes.shape[1], rows), jnp.int32),
            pltpu.VMEM((routes.shape[1], rows), f32),
            pltpu.VMEM((width, hidden), bf16),
            pltpu.VMEM((width, hidden), bf16),
            pltpu.VMEM((hidden, width), bf16),
            pltpu.VMEM((2, 2, 2, rows, width), bf16),
            pltpu.VMEM((2, 2, 2, rows, LANES), bf16),
            pltpu.VMEM((8, part, 2 * piece), bf16),
            pltpu.VMEM((8, part, 2 * piece), bf16),
            pltpu.VMEM((4, part, 2 * piece), bf16),
            pltpu.VMEM((4, part, 2 * piece), bf16),
            pltpu.VMEM((4, 4, part, piece), bf16),
            pltpu.VMEM((4, part, width), f32),
            pltpu.VMEM((CHUNKS, 2, rows, cols), f32),
            pltpu.VMEM((4, CHUNKS, 2, rows, cols), bf16),
            pltpu.VMEM((CHUNKS, nodes - 1, rows, cols), bf16),
            dma((7,)),
            dma((nz - 1,)), dma((2, nz)), dma((nz,)), dma((nodes - 1,)), dma((2, nz)),
            dma((8,)), dma((8,)), dma((4,)), dma((4,)),
            dma((4, 3)), dma((4, 4)),
            dma((CHUNKS, nodes - 1)), dma((CHUNKS, nodes - 1)),
        ],
        compiler_params=pltpu.CompilerParams(
            collective_id=0, has_side_effects=True, vmem_limit_bytes=VMEM_BYTES
        ),
        cost_estimate=pl.CostEstimate(
            flops=6 * total * width * hidden, bytes_accessed=6 * width * hidden, transcendentals=0
        ),
    )(tokens, sign_bits.reshape(1, width), routes.T, gate_values.T, gate_w, up_w, down_w)


def fits_fused(tokens, routes, gate_w, capacity):
    nodes, rows = lax.axis_size("node"), tokens.shape[0]
    return (
        capacity >= rows
        and nodes == 8
        and lax.axis_size("local") == 4
        and rows % 16 == 0
        and nodes * rows <= 256
        and tokens.shape[1] % (CHUNKS * LANES) == 0
        and gate_w.shape[2] % (4 * LANES) == 0
    )


def hadamard_table(block_order):
    kernel_two = jnp.array([[1.0, 1.0], [1.0, -1.0]], jnp.float32)
    matrix = jnp.ones((1, 1), jnp.float32)
    while matrix.shape[0] < block_order:
        matrix = jnp.kron(matrix, kernel_two)
    return matrix / math.sqrt(block_order)


def slot_table(routes, experts, capacity):
    rows_all = routes.shape[0] * routes.shape[1]
    flat_routes = routes.reshape(rows_all)
    onehot = (flat_routes[:, None] == jnp.arange(experts, dtype=jnp.int32)[None, :]).astype(
        jnp.int32
    )
    ranks = jnp.sum(jnp.cumsum(onehot, axis=0) * onehot, axis=1) - 1
    slot_ids = flat_routes * capacity + ranks
    return slot_ids[None, :] == jnp.arange(experts * capacity, dtype=jnp.int32)[:, None]


def per_device(tokens, sign_bits, routes, gate_values, gate_w, up_w, down_w):
    experts = lax.axis_size("node")
    tok_node, width_dev = tokens.shape
    top_count = routes.shape[1]
    capacity = max(2, 2 * tok_node * top_count // experts)
    if fits_fused(tokens, routes, gate_w, capacity):
        return fused(tokens, sign_bits, routes, gate_values, gate_w, up_w, down_w)
    placed = slot_table(routes, experts, capacity).reshape(experts * capacity, tok_node, top_count)
    scatter_mat = jnp.any(placed, axis=2).astype(jnp.bfloat16)
    combine_mat = jnp.sum(placed.astype(jnp.float32) * gate_values[None, :, :], axis=2)
    hadamard = hadamard_table(HB)
    sign_vals = (1 - 2 * sign_bits).astype(jnp.float32)
    signed = tokens.astype(jnp.float32) * sign_vals[None, :]
    block_count = width_dev // HB
    group_size = min(2, block_count)
    group_width = group_size * HB
    received = []
    for group_index in range(block_count // group_size):
        rotated_parts = []
        for inner_index in range(group_size):
            first_col = group_index * group_width + inner_index * HB
            feature_block = signed[:, first_col : first_col + HB]
            rotated_parts.append(
                jnp.dot(feature_block, hadamard, precision=lax.Precision.HIGHEST).astype(
                    jnp.bfloat16
                )
            )
        rotated = jnp.concatenate(rotated_parts, axis=1)
        outgoing = jnp.dot(scatter_mat, rotated, preferred_element_type=jnp.float32).astype(
            jnp.bfloat16
        )
        received.append(lax.all_to_all(outgoing, "node", split_axis=0, concat_axis=0, tiled=True))
    arrived = jnp.concatenate(received, axis=1)
    gate_part = jnp.dot(arrived, gate_w[0], preferred_element_type=jnp.float32)
    up_part = jnp.dot(arrived, up_w[0], preferred_element_type=jnp.float32)
    gate_full, up_full = lax.psum((gate_part, up_part), "local")
    hidden_full = (jax.nn.silu(gate_full) * up_full).astype(jnp.bfloat16)
    expert_sum = jnp.dot(hidden_full, down_w[0], preferred_element_type=jnp.float32)
    expert_out = expert_sum.astype(jnp.bfloat16)
    combine_left = combine_mat.T
    mixed_blocks = []
    for group_index in range(block_count // group_size):
        out_block = expert_out[:, group_index * group_width : (group_index + 1) * group_width]
        returned_rows = lax.all_to_all(out_block, "node", split_axis=0, concat_axis=0, tiled=True)
        mixed_blocks.append(
            jnp.dot(
                combine_left, returned_rows.astype(jnp.float32), precision=lax.Precision.HIGHEST
            )
        )
    return jnp.concatenate(mixed_blocks, axis=1).astype(jnp.bfloat16)


def solution(mesh):
    in_specs = (
        P("node", "local"),
        P("local"),
        P("node", None),
        P("node", None),
        P("node", "local", None),
        P("node", "local", None),
        P("node", None, "local"),
    )
    out_specs = P("node", "local")
    return jax.shard_map(
        per_device, mesh=mesh, in_specs=in_specs, out_specs=out_specs, check_vma=False
    )
```

```python
import functools
import math

import jax
import jax.numpy as jnp
from jax import lax
from jax.experimental import pallas as pl
from jax.experimental.pallas import tpu as pltpu
from jax.sharding import PartitionSpec as P

HB = 128
LANES = 128
CHUNKS = 2
VMEM_BYTES = 63 * 1024 * 1024
MESH = pl.DeviceIdType.MESH


def fused_kernel(
    nodes,
    tok_hbm, sign_hbm, routes_hbm, gv_hbm, gw_hbm, uw_hbm, dw_hbm, out_ref,
    tok_ref, sign_ref, routes_ref, gv_ref, gw, uw, dw, arr, gates,
    core_out, core_in, y_out, y_in, hid, acc, own, back_out, back_in,
    w_sem, ag_send, ag_recv, fw_send, gate_send, gate_recv, core_send, core_recv, y_send, y_recv,
    hid_send, hid_recv, back_send, back_recv,
):
    rows, width = tok_hbm.shape
    nz = nodes // 2
    half = nz * rows
    piece = gw.shape[1] // 4
    sub = piece // 2
    cols = width // CHUNKS
    f32, bf16 = jnp.float32, jnp.bfloat16

    node = lax.axis_index("node")
    local = lax.axis_index("local")
    z, x = node // 2, node % 2
    y, c = local // 2, local % 2
    x_peer = {"node": z * 2 + (1 - x)}
    z_peers = [z + 1 - 2 * (z % 2), (z + 2) % nz, nz - 1 - z]
    core_peer_l, y_peer_l, far_l = y * 2 + (1 - c), (1 - y) * 2 + c, (1 - y) * 2 + (1 - c)
    core_peer, y_peer, far_peer = {"local": core_peer_l}, {"local": y_peer_l}, {"local": far_l}
    same_plane = [{"node": pz * 2 + x} for pz in z_peers]
    other_plane = [{"node": pz * 2 + (1 - x)} for pz in [z] + z_peers]

    barrier = pltpu.get_barrier_semaphore()
    peers = [core_peer, y_peer, x_peer] + same_plane
    for peer in peers:
        pl.semaphore_signal(barrier, inc=1, device_id=peer, device_id_type=MESH)

    loads = []
    for i, (src, dst) in enumerate((
        (tok_hbm, tok_ref), (sign_hbm, sign_ref), (routes_hbm, routes_ref), (gv_hbm, gv_ref),
        (gw_hbm.at[0], gw), (uw_hbm.at[0], uw), (dw_hbm.at[0], dw),
    )):
        load = pltpu.make_async_copy(src, dst, w_sem.at[i])
        load.start()
        loads.append(load)

    row_id = lax.broadcasted_iota(jnp.int32, (HB, HB), 0)
    col_id = lax.broadcasted_iota(jnp.int32, (HB, HB), 1)
    bits = row_id & col_id
    bits = bits ^ (bits >> 4)
    bits = bits ^ (bits >> 2)
    bits = bits ^ (bits >> 1)
    table = (1 - 2 * (bits & 1)).astype(f32).astype(bf16)
    loads[0].wait()
    loads[1].wait()
    signs = (1 - 2 * sign_ref[...]).astype(f32)
    signed = (tok_ref[...].astype(f32) * signs).astype(bf16)
    count = width // HB
    stacked = jnp.concatenate([signed[:, b * HB : (b + 1) * HB] for b in range(count)], axis=0)
    turned = jnp.dot(stacked, table, preferred_element_type=f32) * (1.0 / math.sqrt(HB))
    for b in range(count):
        arr[x, z, :, b * HB : (b + 1) * HB] = turned[b * rows : (b + 1) * rows].astype(bf16)

    pl.semaphore_wait(barrier, len(peers))

    def gather(plane, pz, send_sem, peer):
        return pltpu.make_async_remote_copy(
            src_ref=arr.at[plane, pz], dst_ref=arr.at[plane, pz], send_sem=send_sem,
            recv_sem=ag_recv.at[plane, pz], device_id=peer, device_id_type=MESH,
        )

    sent = []

    def start(copy):
        copy.start()
        sent.append(copy)
        return copy

    def push(src, dst, send_sem, recv_sem, peer):
        return start(pltpu.make_async_remote_copy(
            src_ref=src, dst_ref=dst, send_sem=send_sem, recv_sem=recv_sem,
            device_id=peer, device_id_type=MESH,
        ))

    for i in (1, 2, 0):
        start(gather(x, z, ag_send.at[i], same_plane[i]))
    start(gather(x, z, fw_send.at[nz - 1], x_peer))
    for i, pz in enumerate(z_peers):
        copy = gather(x, pz, fw_send.at[i], x_peer)
        copy.wait_recv()
        start(copy)
    loads[4].wait()
    loads[5].wait()

    planes = (x, 1 - x)
    halves = (((0,),), ((1, 0), (1, 1)))

    def partial_sums(group, p):
        where = pl.ds(pl.multiple_of(p * piece, piece), piece)
        tokens = arr[planes[group]].reshape(half, width)
        gate = jnp.dot(tokens, gw[:, where], preferred_element_type=f32)
        up = jnp.dot(tokens, uw[:, where], preferred_element_type=f32)
        return gate, up

    def to_core(i, group, p):
        gate, up = partial_sums(group, p)
        core_out[i, :, :piece] = gate.astype(bf16)
        core_out[i, :, piece:] = up.astype(bf16)
        return push(core_out.at[i], core_in.at[i], core_send.at[i], core_recv.at[i], core_peer)

    def add_core(i, copy, gate, up):
        copy.wait_recv()
        return gate + core_in[i, :, :piece].astype(f32), up + core_in[i, :, piece:].astype(f32)

    def to_y(group):
        copy = to_core(group, group, far_l)
        gate, up = add_core(group, copy, *partial_sums(group, y_peer_l))
        for s in range(2):
            y_out[group, s, :, :sub] = gate[:, s * sub : (s + 1) * sub].astype(bf16)
            y_out[group, s, :, sub:] = up[:, s * sub : (s + 1) * sub].astype(bf16)
        return [
            push(y_out.at[part], y_in.at[part], y_send.at[group, s], y_recv.at[group, s], y_peer)
            for s, part in enumerate(halves[group])
        ]

    def spread(group, s, p, i, peer):
        part = halves[group][s]
        ref = hid.at[p].at[part]
        return pltpu.make_async_remote_copy(
            src_ref=ref, dst_ref=ref, send_sem=hid_send.at[group, s, i],
            recv_sem=hid_recv.at[group, s, p], device_id=peer, device_id_type=MESH,
        )

    def activate(group, gate, up, over_y):
        share = 2 // len(over_y)
        for s, copy in enumerate(over_y):
            copy.wait_recv()
            for t in range(s * share, (s + 1) * share):
                cut = slice(t * sub, (t + 1) * sub)
                g = gate[:, cut] + y_in[group, t, :, :sub].astype(f32)
                u = up[:, cut] + y_in[group, t, :, sub:].astype(f32)
                hid[local, group, t] = (g / (1.0 + jnp.exp(-g)) * u).astype(bf16)
            for i, peer in enumerate((y_peer, far_peer, core_peer)):
                start(spread(group, s, local, i, peer))

    def wait_hidden(group, p):
        for s in range(len(halves[group])):
            spread(group, s, p, 0, core_peer).wait_recv()

    over_y0 = to_y(0)
    near0 = to_core(2, 0, core_peer_l)
    for pz in [z] + z_peers:
        gather(1 - x, pz, fw_send.at[0], x_peer).wait_recv()
    over_y1 = to_y(1)
    gate0, up0 = partial_sums(0, local)

    activate(0, *add_core(2, near0, gate0, up0), over_y0)
    near1 = to_core(3, 1, core_peer_l)
    gate1, up1 = partial_sums(1, local)

    loads[2].wait()
    loads[3].wait()
    code = lax.broadcasted_iota(jnp.int32, (LANES, rows), 0)
    dense = jnp.zeros((LANES, rows), f32)
    for k in range(routes_ref.shape[0]):
        hit = (code % nodes) == routes_ref[k : k + 1, :]
        dense = dense + jnp.where(hit, gv_ref[k : k + 1, :], 0.0)
    high = dense.astype(bf16).astype(f32)
    middle = (dense - high).astype(bf16).astype(f32)
    low = dense - high - middle
    parts = jnp.where(code < nodes, high, jnp.where(code < 2 * nodes, middle, low))
    parts = jnp.where(code < 3 * nodes, parts, 0.0).astype(bf16)
    same = lax.broadcasted_iota(jnp.int32, (rows, rows), 0) == lax.broadcasted_iota(jnp.int32, (rows, rows), 1)
    turned = lax.dot_general(
        same.astype(f32).astype(bf16), parts, (((1,), (1,)), ((), ())), preferred_element_type=f32
    )
    gates[x, z] = turned.astype(bf16)
    for i, peer in enumerate(same_plane + other_plane):
        push(gates.at[x, z], gates.at[x, z], gate_send.at[i], gate_recv.at[x, z], peer)

    chunk_at = [slice(j * cols, (j + 1) * cols) for j in range(CHUNKS)]

    def down(group, p, where):
        depth = pl.ds(pl.multiple_of(p * piece, piece), piece)
        units = jnp.concatenate([hid[p, group, 0], hid[p, group, 1]], axis=1)
        return jnp.dot(units, dw[depth, where], preferred_element_type=f32)

    lane = lax.broadcasted_iota(jnp.int32, (half, LANES), 1)
    mine = (lane == node) | (lane == node + nodes) | (lane == node + 2 * nodes)

    def begin_down(group):
        for where in chunk_at:
            acc[group, :, where] = down(group, local, where)
        wait_hidden(group, core_peer_l)
        for where in chunk_at:
            acc[group, :, where] += down(group, core_peer_l, where)

    def give_back(group):
        wait_hidden(group, y_peer_l)
        for where in chunk_at:
            acc[group, :, where] += down(group, y_peer_l, where)
        for pz in z_peers + ([z] if group else []):
            pltpu.make_async_remote_copy(
                src_ref=gates.at[x, z], dst_ref=gates.at[planes[group], pz], send_sem=gate_send.at[0],
                recv_sem=gate_recv.at[planes[group], pz], device_id=x_peer, device_id_type=MESH,
            ).wait_recv()
        coded = gates[planes[group]].reshape(half, LANES).astype(f32)
        weight = jnp.sum(jnp.where(mine, coded, 0.0), axis=1, keepdims=True)
        wait_hidden(group, far_l)
        targets = ([z] + z_peers, other_plane) if group else (z_peers, same_plane)
        for j, where in enumerate(chunk_at):
            result = (acc[group, :, where] + down(group, far_l, where)).astype(bf16).astype(f32)
            weighted = (result * weight).reshape(nz, rows, cols)
            back_out[group, j] = weighted.astype(bf16)
            if group == 0:
                own[j] = weighted
            for i in ((2, 3, 1, 0) if group else (1, 2, 0)):
                pz, peer = targets[0][i], targets[1][i]
                slot = i + group * (nz - 1)
                push(back_out.at[group, j, pz], back_in.at[j, slot],
                     back_send.at[j, slot], back_recv.at[j, slot], peer)

    loads[6].wait()
    begin_down(0)
    activate(1, *add_core(3, near1, gate1, up1), over_y1)
    give_back(0)
    begin_down(1)
    give_back(1)
    for copy in sent:
        copy.wait_send()

    for j, where in enumerate(chunk_at):
        mixed = own[j, z]
        for i in range(nodes - 1):
            pltpu.make_async_remote_copy(
                src_ref=back_out.at[0, j, 0], dst_ref=back_in.at[j, i], send_sem=back_send.at[j, i],
                recv_sem=back_recv.at[j, i], device_id=x_peer, device_id_type=MESH,
            ).wait_recv()
            mixed = mixed + back_in[j, i].astype(f32)
        out_ref[:, where] = mixed.astype(bf16)


def fused(tokens, sign_bits, routes, gate_values, gate_w, up_w, down_w):
    nodes = lax.axis_size("node")
    rows, width = tokens.shape
    hidden = gate_w.shape[2]
    nz, piece, cols = nodes // 2, hidden // 4, width // CHUNKS
    total, half = nodes * rows, nz * rows
    bf16, f32 = jnp.bfloat16, jnp.float32
    dma = pltpu.SemaphoreType.DMA
    vmem = pl.BlockSpec(memory_space=pltpu.VMEM)
    hbm = pl.BlockSpec(memory_space=pltpu.HBM)
    return pl.pallas_call(
        functools.partial(fused_kernel, nodes),
        out_shape=pltpu.VMEM((rows, width), bf16),
        in_specs=[hbm] * 7,
        out_specs=vmem,
        scratch_shapes=[
            pltpu.VMEM((rows, width), bf16),
            pltpu.VMEM((1, width), jnp.int32),
            pltpu.VMEM((routes.shape[1], rows), jnp.int32),
            pltpu.VMEM((routes.shape[1], rows), f32),
            pltpu.VMEM((width, hidden), bf16),
            pltpu.VMEM((width, hidden), bf16),
            pltpu.VMEM((hidden, width), bf16),
            pltpu.VMEM((2, nz, rows, width), bf16),
            pltpu.VMEM((2, nz, rows, LANES), bf16),
            pltpu.VMEM((4, half, 2 * piece), bf16),
            pltpu.VMEM((4, half, 2 * piece), bf16),
            pltpu.VMEM((2, 2, half, piece), bf16),
            pltpu.VMEM((2, 2, half, piece), bf16),
            pltpu.VMEM((4, 2, 2, half, piece // 2), bf16),
            pltpu.VMEM((2, half, width), f32),
            pltpu.VMEM((CHUNKS, nz, rows, cols), f32),
            pltpu.VMEM((2, CHUNKS, nz, rows, cols), bf16),
            pltpu.VMEM((CHUNKS, nodes - 1, rows, cols), bf16),
            dma((7,)),
            dma((nz - 1,)), dma((2, nz)), dma((nz,)), dma((nodes - 1,)), dma((2, nz)),
            dma((4,)), dma((4,)), dma((2, 2)), dma((2, 2)),
            dma((2, 2, 3)), dma((2, 2, 4)),
            dma((CHUNKS, nodes - 1)), dma((CHUNKS, nodes - 1)),
        ],
        compiler_params=pltpu.CompilerParams(
            collective_id=0, has_side_effects=True, vmem_limit_bytes=VMEM_BYTES
        ),
        cost_estimate=pl.CostEstimate(
            flops=6 * total * width * hidden, bytes_accessed=6 * width * hidden, transcendentals=0
        ),
    )(tokens, sign_bits.reshape(1, width), routes.T, gate_values.T, gate_w, up_w, down_w)


def fits_fused(tokens, routes, gate_w, capacity):
    nodes, rows = lax.axis_size("node"), tokens.shape[0]
    return (
        capacity >= rows
        and nodes == 8
        and lax.axis_size("local") == 4
        and rows % 16 == 0
        and nodes * rows <= 256
        and tokens.shape[1] % (CHUNKS * LANES) == 0
        and gate_w.shape[2] % (8 * LANES) == 0
    )


def hadamard_table(block_order):
    kernel_two = jnp.array([[1.0, 1.0], [1.0, -1.0]], jnp.float32)
    matrix = jnp.ones((1, 1), jnp.float32)
    while matrix.shape[0] < block_order:
        matrix = jnp.kron(matrix, kernel_two)
    return matrix / math.sqrt(block_order)


def slot_table(routes, experts, capacity):
    rows_all = routes.shape[0] * routes.shape[1]
    flat_routes = routes.reshape(rows_all)
    onehot = (flat_routes[:, None] == jnp.arange(experts, dtype=jnp.int32)[None, :]).astype(
        jnp.int32
    )
    ranks = jnp.sum(jnp.cumsum(onehot, axis=0) * onehot, axis=1) - 1
    slot_ids = flat_routes * capacity + ranks
    return slot_ids[None, :] == jnp.arange(experts * capacity, dtype=jnp.int32)[:, None]


def per_device(tokens, sign_bits, routes, gate_values, gate_w, up_w, down_w):
    experts = lax.axis_size("node")
    tok_node, width_dev = tokens.shape
    top_count = routes.shape[1]
    capacity = max(2, 2 * tok_node * top_count // experts)
    if fits_fused(tokens, routes, gate_w, capacity):
        return fused(tokens, sign_bits, routes, gate_values, gate_w, up_w, down_w)
    placed = slot_table(routes, experts, capacity).reshape(experts * capacity, tok_node, top_count)
    scatter_mat = jnp.any(placed, axis=2).astype(jnp.bfloat16)
    combine_mat = jnp.sum(placed.astype(jnp.float32) * gate_values[None, :, :], axis=2)
    hadamard = hadamard_table(HB)
    sign_vals = (1 - 2 * sign_bits).astype(jnp.float32)
    signed = tokens.astype(jnp.float32) * sign_vals[None, :]
    block_count = width_dev // HB
    group_size = min(2, block_count)
    group_width = group_size * HB
    received = []
    for group_index in range(block_count // group_size):
        rotated_parts = []
        for inner_index in range(group_size):
            first_col = group_index * group_width + inner_index * HB
            feature_block = signed[:, first_col : first_col + HB]
            rotated_parts.append(
                jnp.dot(feature_block, hadamard, precision=lax.Precision.HIGHEST).astype(
                    jnp.bfloat16
                )
            )
        rotated = jnp.concatenate(rotated_parts, axis=1)
        outgoing = jnp.dot(scatter_mat, rotated, preferred_element_type=jnp.float32).astype(
            jnp.bfloat16
        )
        received.append(lax.all_to_all(outgoing, "node", split_axis=0, concat_axis=0, tiled=True))
    arrived = jnp.concatenate(received, axis=1)
    gate_part = jnp.dot(arrived, gate_w[0], preferred_element_type=jnp.float32)
    up_part = jnp.dot(arrived, up_w[0], preferred_element_type=jnp.float32)
    gate_full, up_full = lax.psum((gate_part, up_part), "local")
    hidden_full = (jax.nn.silu(gate_full) * up_full).astype(jnp.bfloat16)
    expert_sum = jnp.dot(hidden_full, down_w[0], preferred_element_type=jnp.float32)
    expert_out = expert_sum.astype(jnp.bfloat16)
    combine_left = combine_mat.T
    mixed_blocks = []
    for group_index in range(block_count // group_size):
        out_block = expert_out[:, group_index * group_width : (group_index + 1) * group_width]
        returned_rows = lax.all_to_all(out_block, "node", split_axis=0, concat_axis=0, tiled=True)
        mixed_blocks.append(
            jnp.dot(
                combine_left, returned_rows.astype(jnp.float32), precision=lax.Precision.HIGHEST
            )
        )
    return jnp.concatenate(mixed_blocks, axis=1).astype(jnp.bfloat16)


def solution(mesh):
    in_specs = (
        P("node", "local"),
        P("local"),
        P("node", None),
        P("node", None),
        P("node", "local", None),
        P("node", "local", None),
        P("node", None, "local"),
    )
    out_specs = P("node", "local")
    return jax.shard_map(
        per_device, mesh=mesh, in_specs=in_specs, out_specs=out_specs, check_vma=False
    )
```

```python
import functools
import math

import jax
import jax.numpy as jnp
from jax import lax
from jax.experimental import pallas as pl
from jax.experimental.pallas import tpu as pltpu
from jax.sharding import PartitionSpec as P

HB = 128
LANES = 128
CHUNKS = 1
VMEM_BYTES = 63 * 1024 * 1024
MESH = pl.DeviceIdType.MESH


def fused_kernel(
    nodes,
    tok_hbm, sign_hbm, routes_hbm, gv_hbm, gw_hbm, uw_hbm, dw_hbm, out_ref,
    tok_ref, sign_ref, routes_ref, gv_ref, gw, uw, dw, arr,
    core_out, core_in, y_out, y_in, hid, acc, own, back_out, back_in,
    w_sem, ag_send, ag_recv, fw_send, fw_recv, core_send, core_recv, y_send, y_recv,
    hid_send, hid_recv, back_send, back_recv,
):
    rows, width = tok_hbm.shape
    nz = nodes // 2
    half = nz * rows
    piece = gw.shape[1] // 4
    cols = width // CHUNKS
    f32, bf16 = jnp.float32, jnp.bfloat16

    node = lax.axis_index("node")
    local = lax.axis_index("local")
    z, x = node // 2, node % 2
    y, c = local // 2, local % 2
    x_peer = {"node": z * 2 + (1 - x)}
    z_peers = [z + 1 - 2 * (z % 2), (z + 2) % nz, nz - 1 - z]
    core_peer_l, y_peer_l, far_l = y * 2 + (1 - c), (1 - y) * 2 + c, (1 - y) * 2 + (1 - c)
    core_peer, y_peer, far_peer = {"local": core_peer_l}, {"local": y_peer_l}, {"local": far_l}
    same_plane = [{"node": pz * 2 + x} for pz in z_peers]
    other_plane = [{"node": pz * 2 + (1 - x)} for pz in [z] + z_peers]

    barrier = pltpu.get_barrier_semaphore()
    peers = [core_peer, y_peer, x_peer] + same_plane
    for peer in peers:
        pl.semaphore_signal(barrier, inc=1, device_id=peer, device_id_type=MESH)

    loads = []
    for i, (src, dst) in enumerate((
        (tok_hbm, tok_ref), (sign_hbm, sign_ref), (routes_hbm, routes_ref), (gv_hbm, gv_ref),
        (gw_hbm.at[0], gw), (uw_hbm.at[0], uw), (dw_hbm.at[0], dw),
    )):
        load = pltpu.make_async_copy(src, dst, w_sem.at[i])
        load.start()
        loads.append(load)

    row_id = lax.broadcasted_iota(jnp.int32, (HB, HB), 0)
    col_id = lax.broadcasted_iota(jnp.int32, (HB, HB), 1)
    bits = row_id & col_id
    bits = bits ^ (bits >> 4)
    bits = bits ^ (bits >> 2)
    bits = bits ^ (bits >> 1)
    table = (1 - 2 * (bits & 1)).astype(f32).astype(bf16)
    loads[0].wait()
    loads[1].wait()
    signs = (1 - 2 * sign_ref[...]).astype(f32)
    signed = (tok_ref[...].astype(f32) * signs).astype(bf16)
    count = width // HB
    stacked = jnp.concatenate([signed[:, b * HB : (b + 1) * HB] for b in range(count)], axis=0)
    turned = jnp.dot(stacked, table, preferred_element_type=f32) * (1.0 / math.sqrt(HB))
    for b in range(count):
        arr[x, z, :, b * HB : (b + 1) * HB] = turned[b * rows : (b + 1) * rows].astype(bf16)

    loads[2].wait()
    loads[3].wait()
    code = lax.broadcasted_iota(jnp.int32, (LANES, rows), 0)
    dense = jnp.zeros((LANES, rows), f32)
    for k in range(routes_ref.shape[0]):
        hit = (code % nodes) == routes_ref[k : k + 1, :]
        dense = dense + jnp.where(hit, gv_ref[k : k + 1, :], 0.0)
    high = dense.astype(bf16).astype(f32)
    middle = (dense - high).astype(bf16).astype(f32)
    low = dense - high - middle
    parts = jnp.where(code < nodes, high, jnp.where(code < 2 * nodes, middle, low))
    parts = jnp.where(code < 3 * nodes, parts, 0.0).astype(bf16)
    same = lax.broadcasted_iota(jnp.int32, (rows, rows), 0) == lax.broadcasted_iota(jnp.int32, (rows, rows), 1)
    turned = lax.dot_general(
        same.astype(f32).astype(bf16), parts, (((1,), (1,)), ((), ())), preferred_element_type=f32
    )
    arr[x, z, :, width:] = turned.astype(bf16)

    pl.semaphore_wait(barrier, len(peers))

    def gather(pz, send_sem, recv_sem, peer):
        return pltpu.make_async_remote_copy(
            src_ref=arr.at[x, pz], dst_ref=arr.at[x, pz], send_sem=send_sem,
            recv_sem=recv_sem, device_id=peer, device_id_type=MESH,
        )

    def wait_all(ref, sem):
        pltpu.make_async_copy(ref, ref, sem).wait()

    def push(src, dst, send_sem, recv_sem, peer):
        copy = pltpu.make_async_remote_copy(
            src_ref=src, dst_ref=dst, send_sem=send_sem, recv_sem=recv_sem,
            device_id=peer, device_id_type=MESH,
        )
        copy.start()
        return copy

    for i in (1, 2, 0):
        gather(z, ag_send.at[0], ag_recv.at[z], same_plane[i]).start()
    gather(z, fw_send.at[0], fw_recv.at[0], x_peer).start()
    for pz in z_peers:
        gather(pz, ag_send.at[0], ag_recv.at[pz], x_peer).wait_recv()
        gather(pz, fw_send.at[0], fw_recv.at[0], x_peer).start()
    loads[4].wait()
    loads[5].wait()

    planes = (x, 1 - x)

    def partial_sums(group, p):
        where = pl.ds(pl.multiple_of(p * piece, piece), piece)
        tokens = arr[planes[group], :, :, :width].reshape(half, width)
        gate = jnp.dot(tokens, gw[:, where], preferred_element_type=f32)
        up = jnp.dot(tokens, uw[:, where], preferred_element_type=f32)
        return gate, up

    def to_core(i, group, p):
        gate, up = partial_sums(group, p)
        core_out[i, :, :piece] = gate.astype(bf16)
        core_out[i, :, piece:] = up.astype(bf16)
        return push(core_out.at[i], core_in.at[i], core_send.at[0], core_recv.at[i], core_peer)

    def add_core(i, copy, gate, up):
        copy.wait_recv()
        return gate + core_in[i, :, :piece].astype(f32), up + core_in[i, :, piece:].astype(f32)

    def to_y(group):
        copy = to_core(group, group, far_l)
        gate, up = add_core(group, copy, *partial_sums(group, y_peer_l))
        y_out[group, :, :piece] = gate.astype(bf16)
        y_out[group, :, piece:] = up.astype(bf16)
        return push(y_out.at[group], y_in.at[group], y_send.at[0], y_recv.at[group], y_peer)

    def spread(group, p, peer):
        return pltpu.make_async_remote_copy(
            src_ref=hid.at[group, p], dst_ref=hid.at[group, p], send_sem=hid_send.at[group],
            recv_sem=hid_recv.at[group, p], device_id=peer, device_id_type=MESH,
        )

    def activate(group, gate, up, over_y):
        over_y.wait_recv()
        gate = gate + y_in[group, :, :piece].astype(f32)
        up = up + y_in[group, :, piece:].astype(f32)
        hid[group, local] = (gate / (1.0 + jnp.exp(-gate)) * up).astype(bf16)
        for peer in (y_peer, far_peer, core_peer):
            spread(group, local, peer).start()

    over_y0 = to_y(0)
    near0 = to_core(2, 0, core_peer_l)
    wait_all(arr.at[1 - x], fw_recv.at[0])
    over_y1 = to_y(1)
    gate0, up0 = partial_sums(0, local)

    activate(0, *add_core(2, near0, gate0, up0), over_y0)
    near1 = to_core(3, 1, core_peer_l)
    gate1, up1 = partial_sums(1, local)
    activate(1, *add_core(3, near1, gate1, up1), over_y1)
    loads[6].wait()

    chunk_at = [slice(j * cols, (j + 1) * cols) for j in range(CHUNKS)]

    def down(group, p, where):
        depth = pl.ds(pl.multiple_of(p * piece, piece), piece)
        return jnp.dot(hid[group, p], dw[depth, where], preferred_element_type=f32)

    lane = lax.broadcasted_iota(jnp.int32, (half, LANES), 1)
    mine = (lane == node) | (lane == node + nodes) | (lane == node + 2 * nodes)

    def give_back(group):
        for where in chunk_at:
            acc[group, :, where] = down(group, local, where)
        for p in (core_peer_l, y_peer_l):
            spread(group, p, core_peer).wait_recv()
            for where in chunk_at:
                acc[group, :, where] += down(group, p, where)
        coded = arr[planes[group], :, :, width:].reshape(half, LANES).astype(f32)
        weight = jnp.sum(jnp.where(mine, coded, 0.0), axis=1, keepdims=True)
        spread(group, far_l, core_peer).wait_recv()
        targets = ([z] + z_peers, other_plane) if group else (z_peers, same_plane)
        for j, where in enumerate(chunk_at):
            result = (acc[group, :, where] + down(group, far_l, where)).astype(bf16).astype(f32)
            weighted = (result * weight).reshape(nz, rows, cols)
            back_out[group, j] = weighted.astype(bf16)
            if group == 0:
                own[j] = weighted
            for i in ((2, 3, 1, 0) if group else (1, 2, 0)):
                pz, peer = targets[0][i], targets[1][i]
                slot = i + group * (nz - 1)
                push(back_out.at[group, j, pz], back_in.at[j, slot],
                     back_send.at[0], back_recv.at[0], peer)

    give_back(0)
    give_back(1)
    wait_all(arr.at[x, : nz - 1], ag_send.at[0])
    wait_all(arr.at[x], fw_send.at[0])
    wait_all(core_out, core_send.at[0])
    wait_all(y_out, y_send.at[0])
    for group in range(2):
        wait_all(hid.at[group, :3], hid_send.at[group])
    wait_all(back_in, back_send.at[0])
    wait_all(back_in, back_recv.at[0])

    for j, where in enumerate(chunk_at):
        mixed = own[j, z]
        for i in range(nodes - 1):
            mixed = mixed + back_in[j, i].astype(f32)
        out_ref[:, where] = mixed.astype(bf16)


def fused(tokens, sign_bits, routes, gate_values, gate_w, up_w, down_w):
    nodes = lax.axis_size("node")
    rows, width = tokens.shape
    hidden = gate_w.shape[2]
    nz, piece, cols = nodes // 2, hidden // 4, width // CHUNKS
    total, half = nodes * rows, nz * rows
    bf16, f32 = jnp.bfloat16, jnp.float32
    dma = pltpu.SemaphoreType.DMA
    vmem = pl.BlockSpec(memory_space=pltpu.VMEM)
    hbm = pl.BlockSpec(memory_space=pltpu.HBM)
    return pl.pallas_call(
        functools.partial(fused_kernel, nodes),
        out_shape=pltpu.VMEM((rows, width), bf16),
        in_specs=[hbm] * 7,
        out_specs=vmem,
        scratch_shapes=[
            pltpu.VMEM((rows, width), bf16),
            pltpu.VMEM((1, width), jnp.int32),
            pltpu.VMEM((routes.shape[1], rows), jnp.int32),
            pltpu.VMEM((routes.shape[1], rows), f32),
            pltpu.VMEM((width, hidden), bf16),
            pltpu.VMEM((width, hidden), bf16),
            pltpu.VMEM((hidden, width), bf16),
            pltpu.VMEM((2, nz, rows, width + LANES), bf16),
            pltpu.VMEM((4, half, 2 * piece), bf16),
            pltpu.VMEM((4, half, 2 * piece), bf16),
            pltpu.VMEM((2, half, 2 * piece), bf16),
            pltpu.VMEM((2, half, 2 * piece), bf16),
            pltpu.VMEM((2, 4, half, piece), bf16),
            pltpu.VMEM((2, half, width), f32),
            pltpu.VMEM((CHUNKS, nz, rows, cols), f32),
            pltpu.VMEM((2, CHUNKS, nz, rows, cols), bf16),
            pltpu.VMEM((CHUNKS, nodes - 1, rows, cols), bf16),
            dma((7,)),
            dma((1,)), dma((nz,)), dma((1,)), dma((1,)),
            dma((1,)), dma((4,)), dma((1,)), dma((2,)),
            dma((2,)), dma((2, 4)),
            dma((1,)), dma((1,)),
        ],
        compiler_params=pltpu.CompilerParams(
            collective_id=0, has_side_effects=True, vmem_limit_bytes=VMEM_BYTES
        ),
        cost_estimate=pl.CostEstimate(
            flops=6 * total * width * hidden, bytes_accessed=6 * width * hidden, transcendentals=0
        ),
    )(tokens, sign_bits.reshape(1, width), routes.T, gate_values.T, gate_w, up_w, down_w)


def fits_fused(tokens, routes, gate_w, capacity):
    nodes, rows = lax.axis_size("node"), tokens.shape[0]
    return (
        capacity >= rows
        and nodes == 8
        and lax.axis_size("local") == 4
        and rows % 16 == 0
        and nodes * rows <= 256
        and tokens.shape[1] % (CHUNKS * LANES) == 0
        and gate_w.shape[2] % (4 * LANES) == 0
    )


def hadamard_table(block_order):
    kernel_two = jnp.array([[1.0, 1.0], [1.0, -1.0]], jnp.float32)
    matrix = jnp.ones((1, 1), jnp.float32)
    while matrix.shape[0] < block_order:
        matrix = jnp.kron(matrix, kernel_two)
    return matrix / math.sqrt(block_order)


def slot_table(routes, experts, capacity):
    rows_all = routes.shape[0] * routes.shape[1]
    flat_routes = routes.reshape(rows_all)
    onehot = (flat_routes[:, None] == jnp.arange(experts, dtype=jnp.int32)[None, :]).astype(
        jnp.int32
    )
    ranks = jnp.sum(jnp.cumsum(onehot, axis=0) * onehot, axis=1) - 1
    slot_ids = flat_routes * capacity + ranks
    return slot_ids[None, :] == jnp.arange(experts * capacity, dtype=jnp.int32)[:, None]


def per_device(tokens, sign_bits, routes, gate_values, gate_w, up_w, down_w):
    experts = lax.axis_size("node")
    tok_node, width_dev = tokens.shape
    top_count = routes.shape[1]
    capacity = max(2, 2 * tok_node * top_count // experts)
    if fits_fused(tokens, routes, gate_w, capacity):
        return fused(tokens, sign_bits, routes, gate_values, gate_w, up_w, down_w)
    placed = slot_table(routes, experts, capacity).reshape(experts * capacity, tok_node, top_count)
    scatter_mat = jnp.any(placed, axis=2).astype(jnp.bfloat16)
    combine_mat = jnp.sum(placed.astype(jnp.float32) * gate_values[None, :, :], axis=2)
    hadamard = hadamard_table(HB)
    sign_vals = (1 - 2 * sign_bits).astype(jnp.float32)
    signed = tokens.astype(jnp.float32) * sign_vals[None, :]
    block_count = width_dev // HB
    group_size = min(2, block_count)
    group_width = group_size * HB
    received = []
    for group_index in range(block_count // group_size):
        rotated_parts = []
        for inner_index in range(group_size):
            first_col = group_index * group_width + inner_index * HB
            feature_block = signed[:, first_col : first_col + HB]
            rotated_parts.append(
                jnp.dot(feature_block, hadamard, precision=lax.Precision.HIGHEST).astype(
                    jnp.bfloat16
                )
            )
        rotated = jnp.concatenate(rotated_parts, axis=1)
        outgoing = jnp.dot(scatter_mat, rotated, preferred_element_type=jnp.float32).astype(
            jnp.bfloat16
        )
        received.append(lax.all_to_all(outgoing, "node", split_axis=0, concat_axis=0, tiled=True))
    arrived = jnp.concatenate(received, axis=1)
    gate_part = jnp.dot(arrived, gate_w[0], preferred_element_type=jnp.float32)
    up_part = jnp.dot(arrived, up_w[0], preferred_element_type=jnp.float32)
    gate_full, up_full = lax.psum((gate_part, up_part), "local")
    hidden_full = (jax.nn.silu(gate_full) * up_full).astype(jnp.bfloat16)
    expert_sum = jnp.dot(hidden_full, down_w[0], preferred_element_type=jnp.float32)
    expert_out = expert_sum.astype(jnp.bfloat16)
    combine_left = combine_mat.T
    mixed_blocks = []
    for group_index in range(block_count // group_size):
        out_block = expert_out[:, group_index * group_width : (group_index + 1) * group_width]
        returned_rows = lax.all_to_all(out_block, "node", split_axis=0, concat_axis=0, tiled=True)
        mixed_blocks.append(
            jnp.dot(
                combine_left, returned_rows.astype(jnp.float32), precision=lax.Precision.HIGHEST
            )
        )
    return jnp.concatenate(mixed_blocks, axis=1).astype(jnp.bfloat16)


def solution(mesh):
    in_specs = (
        P("node", "local"),
        P("local"),
        P("node", None),
        P("node", None),
        P("node", "local", None),
        P("node", "local", None),
        P("node", None, "local"),
    )
    out_specs = P("node", "local")
    return jax.shard_map(
        per_device, mesh=mesh, in_specs=in_specs, out_specs=out_specs, check_vma=False
    )
```

```python
import functools
import math

import jax
import jax.numpy as jnp
from jax import lax
from jax.experimental import pallas as pl
from jax.experimental.pallas import tpu as pltpu
from jax.sharding import PartitionSpec as P

HB = 128
LANES = 128
SPLIT = 4
VMEM_BYTES = 63 * 1024 * 1024
MESH = pl.DeviceIdType.MESH


def fused_kernel(
    nodes,
    tok_hbm, sign_hbm, routes_hbm, gv_hbm, gw_hbm, uw_hbm, dw_hbm, out_ref,
    tok_ref, sign_ref, routes_ref, gv_ref, gw, uw, dw, arr,
    core_out, core_in, y_out, y_in, hid, acc, own, back_out, back_in, lead_out, lead_in, pair_out, pair_in,
    w_sem, ag_send, ag_recv, fw_send, fw_recv, core_send, core_recv, y_send, y_recv,
    hid_send, hid_recv, back_send, back_recv, lead_send, lead_recv, pair_send, pair_recv,
):
    rows, width = tok_hbm.shape
    nz = nodes // 2
    half = nz * rows
    piece = gw.shape[1] // 4
    lead = width // SPLIT
    f32, bf16 = jnp.float32, jnp.bfloat16

    node = lax.axis_index("node")
    local = lax.axis_index("local")
    z, x = node // 2, node % 2
    y, c = local // 2, local % 2
    x_peer = {"node": z * 2 + (1 - x)}
    z_peers = [z + 1 - 2 * (z % 2), (z + 2) % nz, nz - 1 - z]
    core_peer_l, y_peer_l, far_l = y * 2 + (1 - c), (1 - y) * 2 + c, (1 - y) * 2 + (1 - c)
    core_peer, y_peer, far_peer = {"local": core_peer_l}, {"local": y_peer_l}, {"local": far_l}
    same_plane = [{"node": pz * 2 + x} for pz in z_peers]
    other_plane = [{"node": pz * 2 + (1 - x)} for pz in [z] + z_peers]

    barrier = pltpu.get_barrier_semaphore()
    peers = [core_peer, y_peer, x_peer] + same_plane
    for peer in peers:
        pl.semaphore_signal(barrier, inc=1, device_id=peer, device_id_type=MESH)

    loads = []
    for i, (src, dst) in enumerate((
        (tok_hbm, tok_ref), (sign_hbm, sign_ref), (routes_hbm, routes_ref), (gv_hbm, gv_ref),
        (gw_hbm.at[0], gw), (uw_hbm.at[0], uw), (dw_hbm.at[0], dw),
    )):
        load = pltpu.make_async_copy(src, dst, w_sem.at[i])
        load.start()
        loads.append(load)

    row_id = lax.broadcasted_iota(jnp.int32, (HB, HB), 0)
    col_id = lax.broadcasted_iota(jnp.int32, (HB, HB), 1)
    bits = row_id & col_id
    bits = bits ^ (bits >> 4)
    bits = bits ^ (bits >> 2)
    bits = bits ^ (bits >> 1)
    table = (1 - 2 * (bits & 1)).astype(f32).astype(bf16)
    loads[0].wait()
    loads[1].wait()
    signs = (1 - 2 * sign_ref[...]).astype(f32)
    signed = (tok_ref[...].astype(f32) * signs).astype(bf16)
    count = width // HB
    stacked = jnp.concatenate([signed[:, b * HB : (b + 1) * HB] for b in range(count)], axis=0)
    turned = jnp.dot(stacked, table, preferred_element_type=f32) * (1.0 / math.sqrt(HB))
    for b in range(count):
        arr[x, z, :, b * HB : (b + 1) * HB] = turned[b * rows : (b + 1) * rows].astype(bf16)

    loads[2].wait()
    loads[3].wait()
    code = lax.broadcasted_iota(jnp.int32, (LANES, rows), 0)
    dense = jnp.zeros((LANES, rows), f32)
    for k in range(routes_ref.shape[0]):
        hit = (code % nodes) == routes_ref[k : k + 1, :]
        dense = dense + jnp.where(hit, gv_ref[k : k + 1, :], 0.0)
    high = dense.astype(bf16).astype(f32)
    middle = (dense - high).astype(bf16).astype(f32)
    low = dense - high - middle
    parts = jnp.where(code < nodes, high, jnp.where(code < 2 * nodes, middle, low))
    parts = jnp.where(code < 3 * nodes, parts, 0.0).astype(bf16)
    same = lax.broadcasted_iota(jnp.int32, (rows, rows), 0) == lax.broadcasted_iota(jnp.int32, (rows, rows), 1)
    turned = lax.dot_general(
        same.astype(f32).astype(bf16), parts, (((1,), (1,)), ((), ())), preferred_element_type=f32
    )
    arr[x, z, :, width:] = turned.astype(bf16)

    pl.semaphore_wait(barrier, len(peers))

    def gather(pz, send_sem, recv_sem, peer):
        return pltpu.make_async_remote_copy(
            src_ref=arr.at[x, pz], dst_ref=arr.at[x, pz], send_sem=send_sem,
            recv_sem=recv_sem, device_id=peer, device_id_type=MESH,
        )

    def wait_all(ref, sem):
        pltpu.make_async_copy(ref, ref, sem).wait()

    def push(src, dst, send_sem, recv_sem, peer):
        copy = pltpu.make_async_remote_copy(
            src_ref=src, dst_ref=dst, send_sem=send_sem, recv_sem=recv_sem,
            device_id=peer, device_id_type=MESH,
        )
        copy.start()
        return copy

    for i in (1, 2, 0):
        gather(z, ag_send.at[0], ag_recv.at[z], same_plane[i]).start()
    gather(z, fw_send.at[0], fw_recv.at[0], x_peer).start()
    for pz in z_peers:
        gather(pz, ag_send.at[0], ag_recv.at[pz], x_peer).wait_recv()
        gather(pz, fw_send.at[0], fw_recv.at[0], x_peer).start()
    loads[4].wait()
    loads[5].wait()

    planes = (x, 1 - x)

    def partial_sums(group, p):
        where = pl.ds(pl.multiple_of(p * piece, piece), piece)
        tokens = arr[planes[group], :, :, :width].reshape(half, width)
        gate = jnp.dot(tokens, gw[:, where], preferred_element_type=f32)
        up = jnp.dot(tokens, uw[:, where], preferred_element_type=f32)
        return gate, up

    def to_core(i, group, p):
        gate, up = partial_sums(group, p)
        core_out[i, :, :piece] = gate.astype(bf16)
        core_out[i, :, piece:] = up.astype(bf16)
        return push(core_out.at[i], core_in.at[i], core_send.at[0], core_recv.at[i], core_peer)

    def add_core(i, copy, gate, up):
        copy.wait_recv()
        return gate + core_in[i, :, :piece].astype(f32), up + core_in[i, :, piece:].astype(f32)

    def to_y(group):
        copy = to_core(group, group, far_l)
        gate, up = add_core(group, copy, *partial_sums(group, y_peer_l))
        y_out[group, :, :piece] = gate.astype(bf16)
        y_out[group, :, piece:] = up.astype(bf16)
        return push(y_out.at[group], y_in.at[group], y_send.at[0], y_recv.at[group], y_peer)

    def spread(group, p, peer):
        return pltpu.make_async_remote_copy(
            src_ref=hid.at[group, p], dst_ref=hid.at[group, p], send_sem=hid_send.at[group],
            recv_sem=hid_recv.at[group, p], device_id=peer, device_id_type=MESH,
        )

    def activate(group, gate, up, over_y):
        over_y.wait_recv()
        gate = gate + y_in[group, :, :piece].astype(f32)
        up = up + y_in[group, :, piece:].astype(f32)
        hid[group, local] = (gate / (1.0 + jnp.exp(-gate)) * up).astype(bf16)
        for peer in (y_peer, far_peer, core_peer):
            spread(group, local, peer).start()

    over_y0 = to_y(0)
    near0 = to_core(2, 0, core_peer_l)
    wait_all(arr.at[1 - x], fw_recv.at[0])
    over_y1 = to_y(1)
    gate0, up0 = partial_sums(0, local)

    activate(0, *add_core(2, near0, gate0, up0), over_y0)
    near1 = to_core(3, 1, core_peer_l)
    gate1, up1 = partial_sums(1, local)
    activate(1, *add_core(3, near1, gate1, up1), over_y1)
    loads[6].wait()

    chunk_at = [slice(0, lead), slice(lead, width)]

    def down(group, p, where):
        depth = pl.ds(pl.multiple_of(p * piece, piece), piece)
        return jnp.dot(hid[group, p], dw[depth, where], preferred_element_type=f32)

    lane = lax.broadcasted_iota(jnp.int32, (half, LANES), 1)
    mine = (lane == node) | (lane == node + nodes) | (lane == node + 2 * nodes)

    def give_back(group):
        for where in chunk_at:
            acc[group, :, where] = down(group, local, where)
        for p in (core_peer_l, y_peer_l):
            spread(group, p, core_peer).wait_recv()
            for where in chunk_at:
                acc[group, :, where] += down(group, p, where)
        coded = arr[planes[group], :, :, width:].reshape(half, LANES).astype(f32)
        weight = jnp.sum(jnp.where(mine, coded, 0.0), axis=1, keepdims=True)
        spread(group, far_l, core_peer).wait_recv()
        targets = ([z] + z_peers, other_plane) if group else (z_peers, same_plane)
        for j, where in enumerate(chunk_at):
            result = (acc[group, :, where] + down(group, far_l, where)).astype(bf16).astype(f32)
            weighted = (result * weight).reshape(nz, rows, -1)
            if group == 0:
                own[:, :, where] = weighted
            if j == 0:
                if group == 1:
                    lead_out[...] = weighted.astype(bf16)
                    push(lead_out, lead_in, lead_send.at[0], lead_recv.at[0], x_peer)
                continue
            back_out[group] = weighted.astype(bf16)
            for i in ((2, 3, 1, 0) if group else (1, 2, 0)):
                pz, peer = targets[0][i], targets[1][i]
                slot = i + group * (nz - 1)
                push(back_out.at[group, pz], back_in.at[slot], back_send.at[0], back_recv.at[0], peer)

    give_back(0)
    give_back(1)
    wait_all(lead_in, lead_recv.at[0])
    summed = own[:, :, :lead] + lead_in[...].astype(f32)
    own[:, :, :lead] = summed
    pair_out[...] = summed.astype(bf16)
    for i in (1, 2, 0):
        push(pair_out.at[z_peers[i]], pair_in.at[i], pair_send.at[0], pair_recv.at[0], same_plane[i])

    wait_all(arr.at[x, : nz - 1], ag_send.at[0])
    wait_all(arr.at[x], fw_send.at[0])
    wait_all(core_out, core_send.at[0])
    wait_all(y_out, y_send.at[0])
    for group in range(2):
        wait_all(hid.at[group, :3], hid_send.at[group])
    wait_all(back_in, back_send.at[0])
    wait_all(lead_out, lead_send.at[0])
    wait_all(pair_in, pair_send.at[0])
    wait_all(back_in, back_recv.at[0])
    wait_all(pair_in, pair_recv.at[0])

    for where, parts_in in zip(chunk_at, (pair_in, back_in)):
        mixed = own[z, :, where]
        for i in range(parts_in.shape[0]):
            mixed = mixed + parts_in[i].astype(f32)
        out_ref[:, where] = mixed.astype(bf16)


def fused(tokens, sign_bits, routes, gate_values, gate_w, up_w, down_w):
    nodes = lax.axis_size("node")
    rows, width = tokens.shape
    hidden = gate_w.shape[2]
    nz, piece, cols = nodes // 2, hidden // 4, width - width // SPLIT
    total, half = nodes * rows, nz * rows
    bf16, f32 = jnp.bfloat16, jnp.float32
    dma = pltpu.SemaphoreType.DMA
    vmem = pl.BlockSpec(memory_space=pltpu.VMEM)
    hbm = pl.BlockSpec(memory_space=pltpu.HBM)
    return pl.pallas_call(
        functools.partial(fused_kernel, nodes),
        out_shape=pltpu.VMEM((rows, width), bf16),
        in_specs=[hbm] * 7,
        out_specs=vmem,
        scratch_shapes=[
            pltpu.VMEM((rows, width), bf16),
            pltpu.VMEM((1, width), jnp.int32),
            pltpu.VMEM((routes.shape[1], rows), jnp.int32),
            pltpu.VMEM((routes.shape[1], rows), f32),
            pltpu.VMEM((width, hidden), bf16),
            pltpu.VMEM((width, hidden), bf16),
            pltpu.VMEM((hidden, width), bf16),
            pltpu.VMEM((2, nz, rows, width + LANES), bf16),
            pltpu.VMEM((4, half, 2 * piece), bf16),
            pltpu.VMEM((4, half, 2 * piece), bf16),
            pltpu.VMEM((2, half, 2 * piece), bf16),
            pltpu.VMEM((2, half, 2 * piece), bf16),
            pltpu.VMEM((2, 4, half, piece), bf16),
            pltpu.VMEM((2, half, width), f32),
            pltpu.VMEM((nz, rows, width), f32),
            pltpu.VMEM((2, nz, rows, cols), bf16),
            pltpu.VMEM((nodes - 1, rows, cols), bf16),
            pltpu.VMEM((nz, rows, width - cols), bf16),
            pltpu.VMEM((nz, rows, width - cols), bf16),
            pltpu.VMEM((nz, rows, width - cols), bf16),
            pltpu.VMEM((nz - 1, rows, width - cols), bf16),
            dma((7,)),
            dma((1,)), dma((nz,)), dma((1,)), dma((1,)),
            dma((1,)), dma((4,)), dma((1,)), dma((2,)),
            dma((2,)), dma((2, 4)),
            dma((1,)), dma((1,)),
            dma((1,)), dma((1,)), dma((1,)), dma((1,)),
        ],
        compiler_params=pltpu.CompilerParams(
            collective_id=0, has_side_effects=True, vmem_limit_bytes=VMEM_BYTES
        ),
        cost_estimate=pl.CostEstimate(
            flops=6 * total * width * hidden, bytes_accessed=6 * width * hidden, transcendentals=0
        ),
    )(tokens, sign_bits.reshape(1, width), routes.T, gate_values.T, gate_w, up_w, down_w)


def fits_fused(tokens, routes, gate_w, capacity):
    nodes, rows = lax.axis_size("node"), tokens.shape[0]
    return (
        capacity >= rows
        and nodes == 8
        and lax.axis_size("local") == 4
        and rows % 16 == 0
        and nodes * rows <= 256
        and tokens.shape[1] % (SPLIT * LANES) == 0
        and gate_w.shape[2] % (4 * LANES) == 0
    )


def hadamard_table(block_order):
    kernel_two = jnp.array([[1.0, 1.0], [1.0, -1.0]], jnp.float32)
    matrix = jnp.ones((1, 1), jnp.float32)
    while matrix.shape[0] < block_order:
        matrix = jnp.kron(matrix, kernel_two)
    return matrix / math.sqrt(block_order)


def slot_table(routes, experts, capacity):
    rows_all = routes.shape[0] * routes.shape[1]
    flat_routes = routes.reshape(rows_all)
    onehot = (flat_routes[:, None] == jnp.arange(experts, dtype=jnp.int32)[None, :]).astype(
        jnp.int32
    )
    ranks = jnp.sum(jnp.cumsum(onehot, axis=0) * onehot, axis=1) - 1
    slot_ids = flat_routes * capacity + ranks
    return slot_ids[None, :] == jnp.arange(experts * capacity, dtype=jnp.int32)[:, None]


def per_device(tokens, sign_bits, routes, gate_values, gate_w, up_w, down_w):
    experts = lax.axis_size("node")
    tok_node, width_dev = tokens.shape
    top_count = routes.shape[1]
    capacity = max(2, 2 * tok_node * top_count // experts)
    if fits_fused(tokens, routes, gate_w, capacity):
        return fused(tokens, sign_bits, routes, gate_values, gate_w, up_w, down_w)
    placed = slot_table(routes, experts, capacity).reshape(experts * capacity, tok_node, top_count)
    scatter_mat = jnp.any(placed, axis=2).astype(jnp.bfloat16)
    combine_mat = jnp.sum(placed.astype(jnp.float32) * gate_values[None, :, :], axis=2)
    hadamard = hadamard_table(HB)
    sign_vals = (1 - 2 * sign_bits).astype(jnp.float32)
    signed = tokens.astype(jnp.float32) * sign_vals[None, :]
    block_count = width_dev // HB
    group_size = min(2, block_count)
    group_width = group_size * HB
    received = []
    for group_index in range(block_count // group_size):
        rotated_parts = []
        for inner_index in range(group_size):
            first_col = group_index * group_width + inner_index * HB
            feature_block = signed[:, first_col : first_col + HB]
            rotated_parts.append(
                jnp.dot(feature_block, hadamard, precision=lax.Precision.HIGHEST).astype(
                    jnp.bfloat16
                )
            )
        rotated = jnp.concatenate(rotated_parts, axis=1)
        outgoing = jnp.dot(scatter_mat, rotated, preferred_element_type=jnp.float32).astype(
            jnp.bfloat16
        )
        received.append(lax.all_to_all(outgoing, "node", split_axis=0, concat_axis=0, tiled=True))
    arrived = jnp.concatenate(received, axis=1)
    gate_part = jnp.dot(arrived, gate_w[0], preferred_element_type=jnp.float32)
    up_part = jnp.dot(arrived, up_w[0], preferred_element_type=jnp.float32)
    gate_full, up_full = lax.psum((gate_part, up_part), "local")
    hidden_full = (jax.nn.silu(gate_full) * up_full).astype(jnp.bfloat16)
    expert_sum = jnp.dot(hidden_full, down_w[0], preferred_element_type=jnp.float32)
    expert_out = expert_sum.astype(jnp.bfloat16)
    combine_left = combine_mat.T
    mixed_blocks = []
    for group_index in range(block_count // group_size):
        out_block = expert_out[:, group_index * group_width : (group_index + 1) * group_width]
        returned_rows = lax.all_to_all(out_block, "node", split_axis=0, concat_axis=0, tiled=True)
        mixed_blocks.append(
            jnp.dot(
                combine_left, returned_rows.astype(jnp.float32), precision=lax.Precision.HIGHEST
            )
        )
    return jnp.concatenate(mixed_blocks, axis=1).astype(jnp.bfloat16)


def solution(mesh):
    in_specs = (
        P("node", "local"),
        P("local"),
        P("node", None),
        P("node", None),
        P("node", "local", None),
        P("node", "local", None),
        P("node", None, "local"),
    )
    out_specs = P("node", "local")
    return jax.shard_map(
        per_device, mesh=mesh, in_specs=in_specs, out_specs=out_specs, check_vma=False
    )
```

```python
import functools
import math

import jax
import jax.numpy as jnp
from jax import lax
from jax.experimental import pallas as pl
from jax.experimental.pallas import tpu as pltpu
from jax.sharding import PartitionSpec as P

HB = 128
LANES = 128
CHUNKS = 1
VMEM_BYTES = 63 * 1024 * 1024
MESH = pl.DeviceIdType.MESH


def fused_kernel(
    nodes,
    tok_hbm, sign_hbm, routes_hbm, gv_hbm, gw_hbm, uw_hbm, dw_hbm, out_ref,
    tok_ref, sign_ref, routes_ref, gv_ref, gw, uw, dw, arr,
    core_out, core_in, y_out, y_in, hid, acc, own, back_out, back_in,
    w_sem, ag_send, ag_recv, fw_send, fw_recv, core_send, core_recv, y_send, y_recv,
    hid_send, hid_recv, back_send, back_recv,
):
    rows, width = tok_hbm.shape
    nz = nodes // 2
    half = nz * rows
    piece = gw.shape[1] // 4
    cols = width // CHUNKS
    f32, bf16 = jnp.float32, jnp.bfloat16

    node = lax.axis_index("node")
    local = lax.axis_index("local")
    z, x = node // 2, node % 2
    y, c = local // 2, local % 2
    z_peers = [z + 1 - 2 * (z % 2), (z + 2) % nz, nz - 1 - z]
    core_peer_l, y_peer_l, far_l = y * 2 + (1 - c), (1 - y) * 2 + c, (1 - y) * 2 + (1 - c)
    core_peer, y_peer, far_peer = {"local": core_peer_l}, {"local": y_peer_l}, {"local": far_l}
    same_plane = [{"node": pz * 2 + x} for pz in z_peers]
    other_plane = [{"node": pz * 2 + (1 - x)} for pz in [z] + z_peers]

    barrier = pltpu.get_barrier_semaphore()
    peers = [core_peer, y_peer] + same_plane + other_plane
    for peer in peers:
        pl.semaphore_signal(barrier, inc=1, device_id=peer, device_id_type=MESH)

    loads = []
    for i, (src, dst) in enumerate((
        (tok_hbm, tok_ref), (sign_hbm, sign_ref), (routes_hbm, routes_ref), (gv_hbm, gv_ref),
        (gw_hbm.at[0], gw), (uw_hbm.at[0], uw), (dw_hbm.at[0], dw),
    )):
        load = pltpu.make_async_copy(src, dst, w_sem.at[i])
        load.start()
        loads.append(load)

    row_id = lax.broadcasted_iota(jnp.int32, (HB, HB), 0)
    col_id = lax.broadcasted_iota(jnp.int32, (HB, HB), 1)
    bits = row_id & col_id
    bits = bits ^ (bits >> 4)
    bits = bits ^ (bits >> 2)
    bits = bits ^ (bits >> 1)
    table = (1 - 2 * (bits & 1)).astype(f32).astype(bf16)
    loads[0].wait()
    loads[1].wait()
    signs = (1 - 2 * sign_ref[...]).astype(f32)
    signed = (tok_ref[...].astype(f32) * signs).astype(bf16)
    count = width // HB
    stacked = jnp.concatenate([signed[:, b * HB : (b + 1) * HB] for b in range(count)], axis=0)
    turned = jnp.dot(stacked, table, preferred_element_type=f32) * (1.0 / math.sqrt(HB))
    for b in range(count):
        arr[x, z, :, b * HB : (b + 1) * HB] = turned[b * rows : (b + 1) * rows].astype(bf16)

    loads[2].wait()
    loads[3].wait()
    code = lax.broadcasted_iota(jnp.int32, (LANES, rows), 0)
    dense = jnp.zeros((LANES, rows), f32)
    for k in range(routes_ref.shape[0]):
        hit = (code % nodes) == routes_ref[k : k + 1, :]
        dense = dense + jnp.where(hit, gv_ref[k : k + 1, :], 0.0)
    high = dense.astype(bf16).astype(f32)
    middle = (dense - high).astype(bf16).astype(f32)
    low = dense - high - middle
    parts = jnp.where(code < nodes, high, jnp.where(code < 2 * nodes, middle, low))
    parts = jnp.where(code < 3 * nodes, parts, 0.0).astype(bf16)
    same = lax.broadcasted_iota(jnp.int32, (rows, rows), 0) == lax.broadcasted_iota(jnp.int32, (rows, rows), 1)
    turned = lax.dot_general(
        same.astype(f32).astype(bf16), parts, (((1,), (1,)), ((), ())), preferred_element_type=f32
    )
    arr[x, z, :, width:] = turned.astype(bf16)

    pl.semaphore_wait(barrier, len(peers))

    def gather(send_sem, recv_sem, peer):
        pltpu.make_async_remote_copy(
            src_ref=arr.at[x, z], dst_ref=arr.at[x, z], send_sem=send_sem,
            recv_sem=recv_sem, device_id=peer, device_id_type=MESH,
        ).start()

    def wait_all(ref, sem):
        pltpu.make_async_copy(ref, ref, sem).wait()

    def push(src, dst, send_sem, recv_sem, peer):
        copy = pltpu.make_async_remote_copy(
            src_ref=src, dst_ref=dst, send_sem=send_sem, recv_sem=recv_sem,
            device_id=peer, device_id_type=MESH,
        )
        copy.start()
        return copy

    for i in (1, 2, 0):
        gather(ag_send.at[0], ag_recv.at[0], same_plane[i])
    for i in (2, 3, 1, 0):
        gather(fw_send.at[0], fw_recv.at[0], other_plane[i])
    wait_all(arr.at[x, : nz - 1], ag_recv.at[0])
    loads[4].wait()
    loads[5].wait()

    planes = (x, 1 - x)

    def partial_sums(group, p):
        where = pl.ds(pl.multiple_of(p * piece, piece), piece)
        tokens = arr[planes[group], :, :, :width].reshape(half, width)
        gate = jnp.dot(tokens, gw[:, where], preferred_element_type=f32)
        up = jnp.dot(tokens, uw[:, where], preferred_element_type=f32)
        return gate, up

    def to_core(i, group, p):
        gate, up = partial_sums(group, p)
        core_out[i, :, :piece] = gate.astype(bf16)
        core_out[i, :, piece:] = up.astype(bf16)
        return push(core_out.at[i], core_in.at[i], core_send.at[0], core_recv.at[i], core_peer)

    def add_core(i, copy, gate, up):
        copy.wait_recv()
        return gate + core_in[i, :, :piece].astype(f32), up + core_in[i, :, piece:].astype(f32)

    def to_y(group):
        copy = to_core(group, group, far_l)
        gate, up = add_core(group, copy, *partial_sums(group, y_peer_l))
        y_out[group, :, :piece] = gate.astype(bf16)
        y_out[group, :, piece:] = up.astype(bf16)
        return push(y_out.at[group], y_in.at[group], y_send.at[0], y_recv.at[group], y_peer)

    def spread(group, p, peer):
        return pltpu.make_async_remote_copy(
            src_ref=hid.at[group, p], dst_ref=hid.at[group, p], send_sem=hid_send.at[group],
            recv_sem=hid_recv.at[group, p], device_id=peer, device_id_type=MESH,
        )

    def activate(group, gate, up, over_y):
        over_y.wait_recv()
        gate = gate + y_in[group, :, :piece].astype(f32)
        up = up + y_in[group, :, piece:].astype(f32)
        hid[group, local] = (gate / (1.0 + jnp.exp(-gate)) * up).astype(bf16)
        for peer in (y_peer, far_peer, core_peer):
            spread(group, local, peer).start()

    over_y0 = to_y(0)
    near0 = to_core(2, 0, core_peer_l)
    wait_all(arr.at[1 - x], fw_recv.at[0])
    over_y1 = to_y(1)
    gate0, up0 = partial_sums(0, local)

    activate(0, *add_core(2, near0, gate0, up0), over_y0)
    near1 = to_core(3, 1, core_peer_l)
    gate1, up1 = partial_sums(1, local)
    activate(1, *add_core(3, near1, gate1, up1), over_y1)
    loads[6].wait()

    chunk_at = [slice(j * cols, (j + 1) * cols) for j in range(CHUNKS)]

    def down(group, p, where):
        depth = pl.ds(pl.multiple_of(p * piece, piece), piece)
        return jnp.dot(hid[group, p], dw[depth, where], preferred_element_type=f32)

    lane = lax.broadcasted_iota(jnp.int32, (half, LANES), 1)
    mine = (lane == node) | (lane == node + nodes) | (lane == node + 2 * nodes)

    def give_back(group):
        for where in chunk_at:
            acc[group, :, where] = down(group, local, where)
        for p in (core_peer_l, y_peer_l):
            spread(group, p, core_peer).wait_recv()
            for where in chunk_at:
                acc[group, :, where] += down(group, p, where)
        coded = arr[planes[group], :, :, width:].reshape(half, LANES).astype(f32)
        weight = jnp.sum(jnp.where(mine, coded, 0.0), axis=1, keepdims=True)
        spread(group, far_l, core_peer).wait_recv()
        targets = ([z] + z_peers, other_plane) if group else (z_peers, same_plane)
        for j, where in enumerate(chunk_at):
            result = (acc[group, :, where] + down(group, far_l, where)).astype(bf16).astype(f32)
            weighted = (result * weight).reshape(nz, rows, cols)
            back_out[group, j] = weighted.astype(bf16)
            if group == 0:
                own[j] = weighted
            for i in ((2, 3, 1, 0) if group else (1, 2, 0)):
                pz, peer = targets[0][i], targets[1][i]
                slot = i + group * (nz - 1)
                push(back_out.at[group, j, pz], back_in.at[j, slot],
                     back_send.at[0], back_recv.at[0], peer)

    give_back(0)
    give_back(1)
    wait_all(arr.at[x, : nz - 1], ag_send.at[0])
    wait_all(arr.at[x], fw_send.at[0])
    wait_all(core_out, core_send.at[0])
    wait_all(y_out, y_send.at[0])
    for group in range(2):
        wait_all(hid.at[group, :3], hid_send.at[group])
    wait_all(back_in, back_send.at[0])
    wait_all(back_in, back_recv.at[0])

    for j, where in enumerate(chunk_at):
        mixed = own[j, z]
        for i in range(nodes - 1):
            mixed = mixed + back_in[j, i].astype(f32)
        out_ref[:, where] = mixed.astype(bf16)


def fused(tokens, sign_bits, routes, gate_values, gate_w, up_w, down_w):
    nodes = lax.axis_size("node")
    rows, width = tokens.shape
    hidden = gate_w.shape[2]
    nz, piece, cols = nodes // 2, hidden // 4, width // CHUNKS
    total, half = nodes * rows, nz * rows
    bf16, f32 = jnp.bfloat16, jnp.float32
    dma = pltpu.SemaphoreType.DMA
    vmem = pl.BlockSpec(memory_space=pltpu.VMEM)
    hbm = pl.BlockSpec(memory_space=pltpu.HBM)
    return pl.pallas_call(
        functools.partial(fused_kernel, nodes),
        out_shape=pltpu.VMEM((rows, width), bf16),
        in_specs=[hbm] * 7,
        out_specs=vmem,
        scratch_shapes=[
            pltpu.VMEM((rows, width), bf16),
            pltpu.VMEM((1, width), jnp.int32),
            pltpu.VMEM((routes.shape[1], rows), jnp.int32),
            pltpu.VMEM((routes.shape[1], rows), f32),
            pltpu.VMEM((width, hidden), bf16),
            pltpu.VMEM((width, hidden), bf16),
            pltpu.VMEM((hidden, width), bf16),
            pltpu.VMEM((2, nz, rows, width + LANES), bf16),
            pltpu.VMEM((4, half, 2 * piece), bf16),
            pltpu.VMEM((4, half, 2 * piece), bf16),
            pltpu.VMEM((2, half, 2 * piece), bf16),
            pltpu.VMEM((2, half, 2 * piece), bf16),
            pltpu.VMEM((2, 4, half, piece), bf16),
            pltpu.VMEM((2, half, width), f32),
            pltpu.VMEM((CHUNKS, nz, rows, cols), f32),
            pltpu.VMEM((2, CHUNKS, nz, rows, cols), bf16),
            pltpu.VMEM((CHUNKS, nodes - 1, rows, cols), bf16),
            dma((7,)),
            dma((1,)), dma((1,)), dma((1,)), dma((1,)),
            dma((1,)), dma((4,)), dma((1,)), dma((2,)),
            dma((2,)), dma((2, 4)),
            dma((1,)), dma((1,)),
        ],
        compiler_params=pltpu.CompilerParams(
            collective_id=0, has_side_effects=True, vmem_limit_bytes=VMEM_BYTES
        ),
        cost_estimate=pl.CostEstimate(
            flops=6 * total * width * hidden, bytes_accessed=6 * width * hidden, transcendentals=0
        ),
    )(tokens, sign_bits.reshape(1, width), routes.T, gate_values.T, gate_w, up_w, down_w)


def fits_fused(tokens, routes, gate_w, capacity):
    nodes, rows = lax.axis_size("node"), tokens.shape[0]
    return (
        capacity >= rows
        and nodes == 8
        and lax.axis_size("local") == 4
        and rows % 16 == 0
        and nodes * rows <= 256
        and tokens.shape[1] % (CHUNKS * LANES) == 0
        and gate_w.shape[2] % (4 * LANES) == 0
    )


def hadamard_table(block_order):
    kernel_two = jnp.array([[1.0, 1.0], [1.0, -1.0]], jnp.float32)
    matrix = jnp.ones((1, 1), jnp.float32)
    while matrix.shape[0] < block_order:
        matrix = jnp.kron(matrix, kernel_two)
    return matrix / math.sqrt(block_order)


def slot_table(routes, experts, capacity):
    rows_all = routes.shape[0] * routes.shape[1]
    flat_routes = routes.reshape(rows_all)
    onehot = (flat_routes[:, None] == jnp.arange(experts, dtype=jnp.int32)[None, :]).astype(
        jnp.int32
    )
    ranks = jnp.sum(jnp.cumsum(onehot, axis=0) * onehot, axis=1) - 1
    slot_ids = flat_routes * capacity + ranks
    return slot_ids[None, :] == jnp.arange(experts * capacity, dtype=jnp.int32)[:, None]


def per_device(tokens, sign_bits, routes, gate_values, gate_w, up_w, down_w):
    experts = lax.axis_size("node")
    tok_node, width_dev = tokens.shape
    top_count = routes.shape[1]
    capacity = max(2, 2 * tok_node * top_count // experts)
    if fits_fused(tokens, routes, gate_w, capacity):
        return fused(tokens, sign_bits, routes, gate_values, gate_w, up_w, down_w)
    placed = slot_table(routes, experts, capacity).reshape(experts * capacity, tok_node, top_count)
    scatter_mat = jnp.any(placed, axis=2).astype(jnp.bfloat16)
    combine_mat = jnp.sum(placed.astype(jnp.float32) * gate_values[None, :, :], axis=2)
    hadamard = hadamard_table(HB)
    sign_vals = (1 - 2 * sign_bits).astype(jnp.float32)
    signed = tokens.astype(jnp.float32) * sign_vals[None, :]
    block_count = width_dev // HB
    group_size = min(2, block_count)
    group_width = group_size * HB
    received = []
    for group_index in range(block_count // group_size):
        rotated_parts = []
        for inner_index in range(group_size):
            first_col = group_index * group_width + inner_index * HB
            feature_block = signed[:, first_col : first_col + HB]
            rotated_parts.append(
                jnp.dot(feature_block, hadamard, precision=lax.Precision.HIGHEST).astype(
                    jnp.bfloat16
                )
            )
        rotated = jnp.concatenate(rotated_parts, axis=1)
        outgoing = jnp.dot(scatter_mat, rotated, preferred_element_type=jnp.float32).astype(
            jnp.bfloat16
        )
        received.append(lax.all_to_all(outgoing, "node", split_axis=0, concat_axis=0, tiled=True))
    arrived = jnp.concatenate(received, axis=1)
    gate_part = jnp.dot(arrived, gate_w[0], preferred_element_type=jnp.float32)
    up_part = jnp.dot(arrived, up_w[0], preferred_element_type=jnp.float32)
    gate_full, up_full = lax.psum((gate_part, up_part), "local")
    hidden_full = (jax.nn.silu(gate_full) * up_full).astype(jnp.bfloat16)
    expert_sum = jnp.dot(hidden_full, down_w[0], preferred_element_type=jnp.float32)
    expert_out = expert_sum.astype(jnp.bfloat16)
    combine_left = combine_mat.T
    mixed_blocks = []
    for group_index in range(block_count // group_size):
        out_block = expert_out[:, group_index * group_width : (group_index + 1) * group_width]
        returned_rows = lax.all_to_all(out_block, "node", split_axis=0, concat_axis=0, tiled=True)
        mixed_blocks.append(
            jnp.dot(
                combine_left, returned_rows.astype(jnp.float32), precision=lax.Precision.HIGHEST
            )
        )
    return jnp.concatenate(mixed_blocks, axis=1).astype(jnp.bfloat16)


def solution(mesh):
    in_specs = (
        P("node", "local"),
        P("local"),
        P("node", None),
        P("node", None),
        P("node", "local", None),
        P("node", "local", None),
        P("node", None, "local"),
    )
    out_specs = P("node", "local")
    return jax.shard_map(
        per_device, mesh=mesh, in_specs=in_specs, out_specs=out_specs, check_vma=False
    )
```
